128 devices in a mesh: node: 8 (over y_lo, x), feat: 16 (over z, y_hi, core).
Axes of the slice: x: 4, y: 4 (y_hi: 2, y_lo: 2; y = y_hi * 2 + y_lo), z: 4, core: 2. Of those that a mesh axis runs over, the one named last changes fastest.
Arguments:
- features: bfloat16 [128, 65536], P('feat', 'node'), may hold values from -6 to 6
- weight: bfloat16 [128, 256], P(None, 'feat'), may hold values from -0.5 to 0.5
- bias: float32 [256], P('feat'), may hold values from -3 to 3
- tile_values: bfloat16 [8, 8, 48, 128, 128], P('node'), may hold values from -0.25 to 0.25
- tile_rows: int32 [8, 8, 48], P('node'), may hold values from 0 to 63
- tile_cols: int32 [8, 8, 48], P('node'), may hold values from 0 to 63
- tile_count: int32 [8, 8], P('node'), may hold values from 0 to 48, as said below
- cotangent: bfloat16 [256, 65536], P('feat', 'node'), may hold values from -6 to 6
Outputs:
- out_field: bfloat16 [256, 65536], P('feat', 'node')
- grad_features: bfloat16 [128, 65536], P('feat', 'node')
- grad_weight: float32 [128, 256], P(None, 'feat')
- grad_bias: float32 [256], P('feat')
The draws below stay inside these ranges and needn't reach their ends.
Inputs may be any that keep to these rules, and one draw needn't show every extreme that they name: tile_count[i, i] = 48 for every shard i; slots at or beyond tile_count are unused.
All inputs are finite; a program needn't handle non-finite values.
Results may differ from the reference program's by a relative error of at most 0.0075.
Values may be sent and summed in bfloat16 or wider, within the bound.
A program may use at most 64 MiB of HBM per device.

```python
import jax
import jax.numpy as jnp
from jax import lax

IN = 128
HID = 256
TILE = 128
ROW_TILES = 64
TPS = 48
NODES = 65536
N_NODE = 8


def draw_tile_count(key, part):
    key = jax.random.fold_in(key, 7)
    shard_numbers = jnp.arange(N_NODE)
    spacing = jnp.abs(shard_numbers[:, None] - shard_numbers[None, :])
    beside_all = jnp.minimum(spacing, N_NODE - spacing)
    ceiling = TPS // (1 + beside_all) + 1
    counts = jax.random.randint(key, (N_NODE, N_NODE), 0, ceiling)
    return jnp.where(beside_all == 0, TPS, counts).astype(jnp.int32)


def touch_ends(values, own_key, low, largest):
    longest = values.shape.index(max(values.shape))
    spots = []
    for shift in (0, 1):
        where = [jax.random.randint(jax.random.fold_in(own_key, axis), (), 0, length) for axis, length in enumerate(values.shape)]
        where[longest] = (where[longest] + shift) % values.shape[longest]
        spots.append(tuple(where))
    return values.at[spots[0]].set(low).at[spots[1]].set(largest)


def levels(stream_key, dims, cuts, low, top_value):
    loudness = 1.0
    for axis_at, shards_of in cuts:
        steps = jax.random.uniform(jax.random.fold_in(jax.random.fold_in(stream_key, 6), axis_at), (shards_of,), jnp.float32, low / len(cuts), top_value / len(cuts))
        loudness = loudness * jnp.repeat(jnp.exp(steps), dims[axis_at] // shards_of).reshape((-1,) + (1,) * (len(dims) - 1 - axis_at))
    return loudness


def gaussian(stream_key, extent, deviation, most, cuts=(), kind=jnp.bfloat16):
    gain = levels(stream_key, extent, cuts, -0.22, 0.18) if cuts else 1.0
    drawn = jax.random.normal(stream_key, extent, jnp.float32) * deviation * gain
    return jnp.minimum(jnp.maximum(drawn, -most), most).astype(kind)


def setup_inputs(seed: int = 0) -> dict:
    splits = jax.random.split(jax.random.key(seed), 9)
    features = gaussian(splits[0], (IN, NODES), 1.0, 6.0, ((0, 16), (1, 8)))
    weight = gaussian(splits[1], (IN, HID), IN ** -0.5, 0.5, ((1, 16),))
    bias = gaussian(splits[2], (HID,), 0.5, 3.0, ((0, 16),), jnp.float32)
    tile_values = gaussian(splits[3], (N_NODE, N_NODE, TPS, TILE, TILE), (4 * TILE) ** -0.5, 0.25, ((0, 8),))
    tile_rows = touch_ends(jax.random.randint(splits[4], (N_NODE, N_NODE, TPS), 0, ROW_TILES), jax.random.fold_in(splits[4], 1), 0, ROW_TILES - 1).astype(jnp.int32)
    tile_cols = touch_ends(jax.random.randint(splits[5], (N_NODE, N_NODE, TPS), 0, ROW_TILES), jax.random.fold_in(splits[5], 1), 0, ROW_TILES - 1).astype(jnp.int32)
    tile_count = draw_tile_count(jax.random.fold_in(splits[8], 71), 0)
    cotangent = gaussian(splits[7], (HID, NODES), 1.0, 6.0, ((0, 16), (1, 8)))
    return {"features": features, "weight": weight, "bias": bias, "tile_values": tile_values, "tile_rows": tile_rows, "tile_cols": tile_cols, "tile_count": tile_count, "cotangent": cotangent}


def forward_part(source, tile_block, row_list, col_list, amount):
    tile_size = tile_block.shape[-1]
    row_tiles = source.shape[1] // tile_size
    adjacency_blocks = source.astype(jnp.float32).reshape(source.shape[0], row_tiles, tile_size)
    picked = jnp.take(adjacency_blocks, col_list, axis=1)
    block_products = jnp.einsum('ftc,trc->ftr', picked, tile_block.astype(jnp.float32), precision=lax.Precision.HIGHEST)
    usable = jnp.arange(col_list.shape[0]) < amount
    spread_lookup = ((row_list[None, :] == jnp.arange(row_tiles)[:, None]) & usable[None, :]).astype(jnp.float32)
    summed_rows = jnp.einsum('nd,idq->inq', spread_lookup, block_products, precision=lax.Precision.HIGHEST)
    return summed_rows.reshape(source.shape[0], row_tiles * tile_size)


def backward_part(source, tile_block, row_list, col_list, amount):
    tile_size = tile_block.shape[-1]
    row_tiles = source.shape[1] // tile_size
    adjacency_blocks = source.astype(jnp.float32).reshape(source.shape[0], row_tiles, tile_size)
    picked = jnp.take(adjacency_blocks, row_list, axis=1)
    block_products = jnp.einsum('ftr,trc->ftc', picked, tile_block.astype(jnp.float32), precision=lax.Precision.HIGHEST)
    usable = jnp.arange(row_list.shape[0]) < amount
    spread_lookup = ((col_list[None, :] == jnp.arange(row_tiles)[:, None]) & usable[None, :]).astype(jnp.float32)
    summed_rows = jnp.einsum('st,ftc->fsc', spread_lookup, block_products, precision=lax.Precision.HIGHEST)
    return summed_rows.reshape(source.shape[0], row_tiles * tile_size)


def reference(features, weight, bias, tile_values, tile_rows, tile_cols, tile_count, cotangent):
    shard_rows = ROW_TILES * TILE
    projected = jnp.dot(weight.T, features, preferred_element_type=jnp.float32).astype(jnp.bfloat16)
    pieces = []
    for dest in range(N_NODE):
        carried = projected[:, dest * shard_rows:(dest + 1) * shard_rows].astype(jnp.float32)
        for source in range(N_NODE):
            carried = carried + forward_part(projected[:, source * shard_rows:(source + 1) * shard_rows], tile_values[dest, source], tile_rows[dest, source], tile_cols[dest, source], tile_count[dest, source])
        pieces.append(carried)
    preact = jnp.concatenate(pieces, axis=1) + bias.astype(jnp.float32)[:, None]
    out_field = jax.nn.silu(preact).astype(jnp.bfloat16)
    sigmoid_pre = jax.nn.sigmoid(preact)
    grad_pre = (cotangent.astype(jnp.float32) * sigmoid_pre * (1.0 + preact * (1.0 - sigmoid_pre))).astype(jnp.bfloat16)
    pieces = []
    for target in range(N_NODE):
        carried = grad_pre[:, target * shard_rows:(target + 1) * shard_rows].astype(jnp.float32)
        for owner in range(N_NODE):
            carried = carried + backward_part(grad_pre[:, owner * shard_rows:(owner + 1) * shard_rows], tile_values[owner, target], tile_rows[owner, target], tile_cols[owner, target], tile_count[owner, target])
        pieces.append(carried)
    grad_proj = jnp.concatenate(pieces, axis=1).astype(jnp.bfloat16)
    grad_features = jnp.dot(weight, grad_proj, preferred_element_type=jnp.float32).astype(jnp.bfloat16)
    normalizer = NODES ** -0.5
    grad_weight = jnp.dot(features, grad_proj.T, preferred_element_type=jnp.float32) * normalizer
    grad_bias = jnp.sum(grad_pre.astype(jnp.float32), axis=1) * normalizer
    return out_field, grad_features, grad_weight, grad_bias
```

```python
import functools

import jax
import jax.numpy as jnp
from jax import lax
from jax.experimental import pallas as pl
from jax.experimental.pallas import tpu as pltpu
from jax.sharding import PartitionSpec as P

MESH = pl.DeviceIdType.MESH
VMEM = pltpu.VMEM
BF16 = jnp.bfloat16
F32 = jnp.float32
TILE = 128
GROUP = 8


def around():
    n, f = lax.axis_index("node"), lax.axis_index("feat")
    nx = lax.axis_size("node") // 2
    x, y = lax.rem(n, nx), n // nx

    def at(dx, dy):
        return (lax.rem(y + dy, 2)) * nx + lax.rem(x + dx + nx, nx)

    return n, f, at


def remote(src, dst, send, recv, node, feat):
    return pltpu.make_async_remote_copy(
        src_ref=src, dst_ref=dst, send_sem=send, recv_sem=recv, device_id=(node, feat), device_id_type=MESH
    )


def greet(n, f, nodes, n_feat):
    barrier = pltpu.get_barrier_semaphore()
    for d in range(1, n_feat):
        pl.semaphore_signal(barrier, inc=1, device_id=(n, lax.rem(f + d, n_feat)), device_id_type=MESH)
    for m in nodes:
        pl.semaphore_signal(barrier, inc=1, device_id=(m, f), device_id_type=MESH)
    pl.semaphore_wait(barrier, n_feat - 1 + len(nodes))


def gather_kernel(
    x_ref, w_ref, proj_ref, fin_out, wt_out, fin, wts, pst,
    w_send, w_recv, x_send, x_recv, p_send, p_recv, own_sem, n_send, n_recv,
):
    n, f, at = around()
    n_feat = fin.shape[0]
    span = fin.shape[2]
    per = pst.shape[1]
    channels = pst.shape[2]
    half = proj_ref.shape[1] // 2
    right, left, other = at(1, 0), at(-1, 0), at(0, 1)

    greet(n, f, (right, left, other), n_feat)

    def cols(p):
        return pl.ds(pl.multiple_of(p * span, span), span)

    wts[f] = w_ref[...].astype(F32).T.astype(BF16)
    sent = []
    for d in range(1, n_feat):
        p = lax.rem(f + d, n_feat)
        sent.append(remote(wts.at[f], wts.at[f], w_send.at[d], w_recv.at[d], n, p))
        sent[-1].start()
        sent.append(remote(x_ref.at[:, cols(p)], fin.at[f], x_send.at[d], x_recv.at[d], n, p))
        sent[-1].start()
    fin[f] = x_ref[:, cols(f)]
    for d in range(1, n_feat):
        p = lax.rem(f - d + n_feat, n_feat)
        remote(wts.at[p], wts.at[p], w_send.at[d], w_recv.at[d], n, p).wait_recv()
        remote(fin.at[p], fin.at[p], x_send.at[d], x_recv.at[d], n, p).wait_recv()

    xin = fin[...].astype(F32).reshape(n_feat * fin.shape[1], span).astype(BF16)
    wt = wts[...].reshape(n_feat * channels, wts.shape[2])
    fin_out[...] = xin
    wt_out[...] = wt
    proj = jnp.dot(wt, xin, preferred_element_type=F32).astype(BF16)
    for p in range(n_feat):
        for t in range(per):
            pst[p, t] = proj[p * channels:(p + 1) * channels, t * TILE:(t + 1) * TILE]

    for d in range(1, n_feat):
        p = lax.rem(f + d, n_feat)
        sent.append(remote(pst.at[p], proj_ref.at[n, pl.ds(f * per, per)], p_send.at[d], p_recv.at[d], n, p))
        sent[-1].start()
    mine = pltpu.make_async_copy(pst.at[f], proj_ref.at[n, pl.ds(f * per, per)], own_sem)
    mine.start()
    for d in range(1, n_feat):
        p = lax.rem(f - d + n_feat, n_feat)
        piece = proj_ref.at[n, pl.ds(p * per, per)]
        remote(piece, piece, p_send.at[d], p_recv.at[d], n, p).wait_recv()
    mine.wait()

    def whole(m):
        return proj_ref.at[m]

    def first(m):
        return proj_ref.at[m, pl.ds(0, half)]

    def second(m):
        return proj_ref.at[m, pl.ds(half, half)]

    def push(block, k, to):
        sent.append(remote(block, block, n_send.at[k], n_recv.at[k], to, f))
        sent[-1].start()

    def arrived(block, k):
        remote(block, block, n_send.at[k], n_recv.at[k], other, f).wait_recv()

    push(whole(n), 0, right)
    push(whole(n), 1, left)
    push(whole(n), 2, other)
    arrived(whole(left), 0)
    push(first(left), 3, right)
    arrived(whole(right), 1)
    push(second(right), 4, left)
    arrived(whole(other), 2)
    push(whole(other), 5, right)
    push(whole(other), 6, left)
    far = at(2, 0)
    arrived(first(far), 3)
    push(first(far), 7, other)
    arrived(second(far), 4)
    push(second(far), 8, other)
    arrived(whole(at(-1, 1)), 5)
    arrived(whole(at(1, 1)), 6)
    arrived(first(at(2, 1)), 7)
    arrived(second(at(2, 1)), 8)
    for copy in sent:
        copy.wait_send()


def layer_kernel(
    count_ref, rows_ref, cols_ref, bias_ref, cot_ref, proj_ref, tiles_ref,
    out_ref, part_ref, own_ref, gbias_ref,
    proj, tiles, acc, gpre, proj_sem, tile_sem,
):
    n = lax.axis_index("node")
    n_node, slots = tiles.shape[0], tiles.shape[1]
    row_tiles, channels = acc.shape[0], acc.shape[1]

    def shard(s):
        return lax.rem(n + s, n_node)

    def chunks(j):
        return (count_ref[j] + (GROUP - 1)) // GROUP

    def proj_copy(j):
        return pltpu.make_async_copy(proj_ref.at[j], proj.at[j], proj_sem.at[j])

    def tile_copy(j, c):
        span = pl.ds(c * GROUP, GROUP)
        return pltpu.make_async_copy(tiles_ref.at[j, span], tiles.at[j, span], tile_sem.at[j, c])

    @pl.loop(0, n_node)
    def _(s):
        j = shard(s)
        proj_copy(j).start()

        @pl.loop(0, chunks(j))
        def _(c):
            tile_copy(j, c).start()

    def products(j, c, source, index_ref, dims):
        made = []
        for u in range(GROUP):
            k = c * GROUP + u
            x = source(j, index_ref[j * slots + k])
            x = jnp.where(k < count_ref[j], x, jnp.zeros_like(x))
            made.append(lax.dot_general(x, tiles[j, k], (dims, ((), ())), preferred_element_type=F32))
        return made

    proj_copy(n).wait()
    bias = jnp.broadcast_to(bias_ref[...], (TILE, channels)).T
    for t in range(row_tiles):
        acc[t] = proj[n, t].astype(F32) + bias

    @pl.loop(0, n_node)
    def _(s):
        j = shard(s)

        @pl.when(s > 0)
        def _():
            proj_copy(j).wait()

        @pl.loop(0, chunks(j))
        def _(c):
            tile_copy(j, c).wait()
            made = products(j, c, lambda j, t: proj[j, t], cols_ref, ((1,), (1,)))
            for u in range(GROUP):
                r = rows_ref[j * slots + c * GROUP + u]
                acc[r] = acc[r] + made[u]

    total = jnp.zeros((channels, TILE), F32)
    for t in range(row_tiles):
        span = slice(t * TILE, (t + 1) * TILE)
        v = acc[t]
        s = jax.nn.sigmoid(v)
        out_ref[:, span] = (v * s).astype(BF16)
        g = (cot_ref[:, span].astype(F32) * s * (1.0 + v * (1.0 - s))).astype(BF16)
        gpre[t] = g
        wide = g.astype(F32)
        own_ref[t] = wide
        total = total + wide
    gbias_ref[...] = total

    def spread(j, target):
        @pl.loop(0, chunks(j))
        def _(c):
            made = products(j, c, lambda j, t: gpre[t], rows_ref, ((1,), (0,)))
            for u in range(GROUP):
                r = cols_ref[j * slots + c * GROUP + u]
                target[r] = target[r] + made[u]

    @pl.loop(1, n_node)
    def _(s):
        j = shard(s)
        acc[...] = jnp.zeros_like(acc)
        spread(j, acc)
        part_ref[j] = acc[...].astype(BF16)

    spread(n, own_ref)
    part_ref[n] = jnp.zeros(part_ref.shape[1:], BF16)


def reduce_kernel(
    norm, part_ref, own_ref, gbias_ref, fin_ref, wt_ref,
    gf_ref, gw_ref, gb_ref,
    far_in, dl_in, dr_in, hl_in, hr_in, fl_in, fr_in, fy_in,
    far_out, y_out, r_out, l_out, gp, gall, gst, wst, wall, nst, nall, ball,
    n_send, n_recv, b_send, b_recv, g_send, g_recv, f_send, f_recv, w_send, w_recv, a_send, a_recv, own_sem,
):
    n, f, at = around()
    n_node = part_ref.shape[0]
    half = part_ref.shape[1] // 2
    n_feat, per, channels = gall.shape[0], gall.shape[1], gall.shape[2]
    span = gst.shape[2]
    right, left, other = at(1, 0), at(-1, 0), at(0, 1)
    others = [lax.rem(n + d, n_node) for d in range(1, n_node)]

    greet(n, f, others, n_feat)

    sent = []

    def push(src, dst, send, recv, node, feat):
        sent.append(remote(src, dst, send, recv, node, feat))
        sent[-1].start()

    def arrived(dst, send, recv):
        remote(dst, dst, send, recv, other, f).wait_recv()

    def add(*terms):
        total = terms[0].astype(F32)
        for term in terms[1:]:
            total = total + term.astype(F32)
        return total

    push(part_ref.at[at(2, 1)], far_in, n_send.at[0], n_recv.at[0], other, f)
    push(part_ref.at[at(1, 1)], dl_in, n_send.at[1], n_recv.at[1], right, f)
    push(part_ref.at[at(-1, 1)], dr_in, n_send.at[2], n_recv.at[2], left, f)
    ball[n] = gbias_ref[...]
    for d in range(1, n_node):
        push(gbias_ref, ball.at[n], b_send.at[d], b_recv.at[d], others[d - 1], f)

    arrived(far_in, n_send.at[0], n_recv.at[0])
    far_out[...] = add(part_ref[at(2, 0)], far_in[...]).astype(BF16)
    push(far_out.at[pl.ds(0, half)], hl_in, n_send.at[3], n_recv.at[3], right, f)
    push(far_out.at[pl.ds(half, half)], hr_in, n_send.at[4], n_recv.at[4], left, f)
    arrived(dl_in, n_send.at[1], n_recv.at[1])
    arrived(dr_in, n_send.at[2], n_recv.at[2])
    y_out[...] = add(part_ref[other], dl_in[...], dr_in[...]).astype(BF16)
    push(y_out, fy_in, n_send.at[5], n_recv.at[5], other, f)
    arrived(hl_in, n_send.at[3], n_recv.at[3])
    r_out[pl.ds(0, half)] = add(part_ref[right, pl.ds(0, half)], hl_in[...]).astype(BF16)
    r_out[pl.ds(half, half)] = part_ref[right, pl.ds(half, half)]
    push(r_out, fl_in, n_send.at[6], n_recv.at[6], right, f)
    arrived(hr_in, n_send.at[4], n_recv.at[4])
    l_out[pl.ds(0, half)] = part_ref[left, pl.ds(0, half)]
    l_out[pl.ds(half, half)] = add(part_ref[left, pl.ds(half, half)], hr_in[...]).astype(BF16)
    push(l_out, fr_in, n_send.at[7], n_recv.at[7], left, f)
    arrived(fy_in, n_send.at[5], n_recv.at[5])
    arrived(fl_in, n_send.at[6], n_recv.at[6])
    arrived(fr_in, n_send.at[7], n_recv.at[7])
    gp[...] = add(own_ref[...], fl_in[...], fr_in[...], fy_in[...]).astype(BF16)

    for d in range(1, n_feat):
        p = lax.rem(f + d, n_feat)
        push(gp.at[pl.ds(p * per, per)], gall.at[f], g_send.at[d], g_recv.at[d], n, p)
    gall[f] = gp[pl.ds(f * per, per)]
    for d in range(1, n_feat):
        p = lax.rem(f - d + n_feat, n_feat)
        arrived(gall.at[p], g_send.at[d], g_recv.at[d])

    hidden = n_feat * channels
    g = jnp.concatenate([gall[:, t].reshape(hidden, TILE) for t in range(per)], axis=1)
    gf = lax.dot_general(wt_ref[...], g, (((0,), (0,)), ((), ())), preferred_element_type=F32)
    rows = gst.shape[1]
    for p in range(n_feat):
        gst[p] = gf[p * rows:(p + 1) * rows].astype(BF16)

    def cols(p):
        return pl.ds(pl.multiple_of(p * span, span), span)

    for d in range(1, n_feat):
        p = lax.rem(f + d, n_feat)
        push(gst.at[p], gf_ref.at[:, cols(f)], f_send.at[d], f_recv.at[d], n, p)
    mine = pltpu.make_async_copy(gst.at[f], gf_ref.at[:, cols(f)], own_sem)
    mine.start()

    gw = lax.dot_general(g, fin_ref[...], (((1,), (1,)), ((), ())), preferred_element_type=F32) * norm
    wst[...] = gw.reshape(wst.shape)
    for d in range(1, n_feat):
        p = lax.rem(f + d, n_feat)
        push(wst.at[p], wall.at[f], w_send.at[d], w_recv.at[d], n, p)
    wall[f] = wst[f]
    for d in range(1, n_feat):
        p = lax.rem(f - d + n_feat, n_feat)
        arrived(wall.at[p], w_send.at[d], w_recv.at[d])
    nst[...] = jnp.sum(wall[...], axis=0)
    for d in range(1, n_node):
        push(nst, nall.at[n], a_send.at[d], a_recv.at[d], others[d - 1], f)
    nall[n] = nst[...]
    for d in range(1, n_node):
        m = lax.rem(n - d + n_node, n_node)
        arrived(ball.at[m], b_send.at[d], b_recv.at[d])
        arrived(nall.at[m], a_send.at[d], a_recv.at[d])
    gw_ref[...] = jnp.sum(nall[...], axis=0).T
    gb_ref[...] = jnp.sum(jnp.sum(ball[...], axis=0).T, axis=0, keepdims=True) * norm
    for d in range(1, n_feat):
        p = lax.rem(f - d + n_feat, n_feat)
        arrived(gf_ref.at[:, cols(p)], f_send.at[d], f_recv.at[d])
    mine.wait()
    for copy in sent:
        copy.wait_send()


def local(features, weight, bias, tile_values, tile_rows, tile_cols, tile_count, cotangent):
    n_node, n_feat = lax.axis_size("node"), lax.axis_size("feat")
    rows, nodes = features.shape
    inputs, channels = weight.shape
    hidden = channels * n_feat
    row_tiles = nodes // TILE
    per = row_tiles // n_feat
    span = per * TILE
    slots = tile_rows.shape[2]
    dma = pltpu.SemaphoreType.DMA
    in_vmem = pl.BlockSpec(memory_space=VMEM)
    in_smem = pl.BlockSpec(memory_space=pltpu.SMEM)
    anywhere = pl.BlockSpec(memory_space=pl.ANY)
    block = (row_tiles, channels, TILE)

    proj, fin, wt = pl.pallas_call(
        gather_kernel,
        out_shape=(
            jax.ShapeDtypeStruct((n_node,) + block, BF16),
            jax.ShapeDtypeStruct((inputs, span), BF16),
            jax.ShapeDtypeStruct((hidden, inputs), BF16),
        ),
        in_specs=[in_vmem] * 2,
        out_specs=(anywhere, in_vmem, in_vmem),
        scratch_shapes=[
            VMEM((n_feat, rows, span), BF16),
            VMEM((n_feat, channels, inputs), BF16),
            VMEM((n_feat, per, channels, TILE), BF16),
        ] + [dma((n_feat,))] * 6 + [dma(()), dma((9,)), dma((9,))],
        compiler_params=pltpu.CompilerParams(
            collective_id=0, has_side_effects=True, vmem_limit_bytes=16 << 20
        ),
        name="gather",
    )(features, weight)

    out, part, own, gbias = pl.pallas_call(
        layer_kernel,
        out_shape=(
            jax.ShapeDtypeStruct((channels, nodes), BF16),
            jax.ShapeDtypeStruct((n_node,) + block, BF16),
            jax.ShapeDtypeStruct(block, F32),
            jax.ShapeDtypeStruct((channels, TILE), F32),
        ),
        in_specs=[in_smem] * 3 + [in_vmem] * 2 + [anywhere] * 2,
        out_specs=(in_vmem,) * 4,
        scratch_shapes=[
            VMEM((n_node,) + block, BF16),
            VMEM((n_node, slots, TILE, TILE), BF16),
            VMEM(block, F32),
            VMEM(block, BF16),
            dma((n_node,)),
            dma((n_node, slots // GROUP)),
        ],
        compiler_params=pltpu.CompilerParams(vmem_limit_bytes=40 << 20),
        name="layer",
    )(
        tile_count.reshape(-1), tile_rows.reshape(-1), tile_cols.reshape(-1),
        bias.reshape(1, channels), cotangent, proj, tile_values[0],
    )

    def blocks(k):
        return [VMEM(block, BF16)] * k

    half = (row_tiles // 2,) + block[1:]
    gf, gw, gb = pl.pallas_call(
        functools.partial(reduce_kernel, 1.0 / float(nodes * n_node) ** 0.5),
        out_shape=(
            jax.ShapeDtypeStruct((rows, nodes), BF16),
            jax.ShapeDtypeStruct((inputs, channels), F32),
            jax.ShapeDtypeStruct((1, channels), F32),
        ),
        in_specs=[in_vmem] * 5,
        out_specs=(anywhere, in_vmem, in_vmem),
        scratch_shapes=blocks(3) + [VMEM(half, BF16)] * 2 + blocks(8) + [
            VMEM((n_feat, per, channels, TILE), BF16),
            VMEM((n_feat, rows, span), BF16),
            VMEM((n_feat, channels, inputs), F32),
            VMEM((n_feat, channels, inputs), F32),
            VMEM((channels, inputs), F32),
            VMEM((n_node, channels, inputs), F32),
            VMEM((n_node, channels, TILE), F32),
            dma((8,)), dma((8,)), dma((n_node,)), dma((n_node,)),
        ] + [dma((n_feat,))] * 6 + [dma((n_node,)), dma((n_node,)), dma(())],
        compiler_params=pltpu.CompilerParams(
            collective_id=1, has_side_effects=True, vmem_limit_bytes=24 << 20
        ),
        name="reduce",
    )(part, own, gbias, fin, wt)
    return out, gf, gw, gb.reshape(channels)


def solution(mesh):
    return jax.shard_map(
        local,
        mesh=mesh,
        in_specs=(
            P("feat", "node"),
            P(None, "feat"),
            P("feat"),
            P("node", None, None, None, None),
            P("node", None, None),
            P("node", None, None),
            P("node", None),
            P("feat", "node"),
        ),
        out_specs=(P("feat", "node"), P("feat", "node"), P(None, "feat"), P("feat")),
        check_vma=False,
    )
```

```python
import functools

import jax
import jax.numpy as jnp
from jax import lax
from jax.experimental import pallas as pl
from jax.experimental.pallas import tpu as pltpu
from jax.sharding import PartitionSpec as P

MESH = pl.DeviceIdType.MESH
VMEM = pltpu.VMEM
BF16 = jnp.bfloat16
F32 = jnp.float32
TILE = 128
GROUP = 8


def around():
    n, f = lax.axis_index("node"), lax.axis_index("feat")
    nx = lax.axis_size("node") // 2
    x, y = lax.rem(n, nx), n // nx

    def at(dx, dy):
        return (lax.rem(y + dy, 2)) * nx + lax.rem(x + dx + nx, nx)

    return n, f, at


def remote(src, dst, send, recv, node, feat):
    return pltpu.make_async_remote_copy(
        src_ref=src, dst_ref=dst, send_sem=send, recv_sem=recv, device_id=(node, feat), device_id_type=MESH
    )


def greet(places):
    barrier = pltpu.get_barrier_semaphore()
    for place in places:
        pl.semaphore_signal(barrier, inc=1, device_id=place, device_id_type=MESH)
    pl.semaphore_wait(barrier, len(places))


def lanes(t, width):
    return pl.ds(pl.multiple_of(t * width, width), width)


class Sender:
    def __init__(self):
        self.sent = []

    def push(self, src, dst, send, recv, node, feat):
        self.sent.append(remote(src, dst, send, recv, node, feat))
        self.sent[-1].start()

    def arrived(self, dst, send, recv):
        remote(dst, dst, send, recv, lax.axis_index("node"), lax.axis_index("feat")).wait_recv()

    def finish(self):
        for copy in self.sent:
            copy.wait_send()


def gather_kernel(x_ref, all_ref, own_sem, send, recv):
    n, f, at = around()
    half = x_ref.shape[1] // 2
    right, left, other, far = at(1, 0), at(-1, 0), at(0, 1), at(2, 0)
    link = Sender()
    greet([(right, f), (left, f), (other, f)])

    def whole(m):
        return all_ref.at[m]

    def first(m):
        return all_ref.at[m, :, pl.ds(0, half)]

    def second(m):
        return all_ref.at[m, :, pl.ds(half, half)]

    def push(block, k, to, src=None):
        link.push(block if src is None else src, block, send.at[k], recv.at[k], to, f)

    def arrived(block, k):
        link.arrived(block, send.at[k], recv.at[k])

    push(whole(n), 0, right, x_ref)
    push(whole(n), 1, left, x_ref)
    push(whole(n), 2, other, x_ref)
    mine = pltpu.make_async_copy(x_ref, whole(n), own_sem)
    mine.start()
    arrived(whole(left), 0)
    push(first(left), 3, right)
    arrived(whole(right), 1)
    push(second(right), 4, left)
    arrived(whole(other), 2)
    push(whole(other), 5, right)
    push(whole(other), 6, left)
    arrived(first(far), 3)
    push(first(far), 7, other)
    arrived(second(far), 4)
    push(second(far), 8, other)
    arrived(whole(at(-1, 1)), 5)
    arrived(whole(at(1, 1)), 6)
    arrived(first(at(2, 1)), 7)
    arrived(second(at(2, 1)), 8)
    mine.wait()
    link.finish()


def tile_stream(count, tiles_ref, tiles, sems):
    def chunks(j):
        return (count[0, j] + (GROUP - 1)) // GROUP

    def copy(j, c):
        span = pl.ds(c * GROUP, GROUP)
        return pltpu.make_async_copy(tiles_ref.at[j, span], tiles.at[j, span], sems.at[j, c])

    return chunks, copy


def products(count, index_ref, tiles, source, j, c, dims):
    made = []
    for u in range(GROUP):
        k = c * GROUP + u
        x = source(index_ref[0, j, k])
        x = jnp.where(k < count[0, j], x, jnp.zeros_like(x))
        made.append(lax.dot_general(x, tiles[j, k], (dims, ((), ())), preferred_element_type=F32))
    return made


def forward_kernel(count, rows, cols, x_ref, tiles_ref, z_ref, tiles, acc, sems):
    n = lax.axis_index("node")
    n_node = tiles.shape[0]
    chunks, copy = tile_stream(count, tiles_ref, tiles, sems)

    @pl.loop(0, n_node)
    def _(s):
        j = lax.rem(n + s, n_node)

        @pl.loop(0, chunks(j))
        def _(c):
            copy(j, c).start()

    for t in range(acc.shape[0]):
        acc[t] = x_ref[n, :, t * TILE:(t + 1) * TILE].astype(F32)

    @pl.loop(0, n_node)
    def _(s):
        j = lax.rem(n + s, n_node)

        @pl.loop(0, chunks(j))
        def _(c):
            copy(j, c).wait()
            made = products(
                count, cols, tiles, lambda t: x_ref[j, :, lanes(t, TILE)], j, c, ((1,), (1,))
            )
            for u in range(GROUP):
                r = rows[0, j, c * GROUP + u]
                acc[r] = acc[r] + made[u]

    for t in range(acc.shape[0]):
        z_ref[:, t * TILE:(t + 1) * TILE] = acc[t].astype(BF16)


def dense_kernel(
    norm, z_ref, cot_ref, wt_ref, bias_ref,
    h_ref, out_ref, gw_ref,
    zin, cin, win, wst, hst, ost, gst, gin,
    z_send, z_recv, c_send, c_recv, w_send, w_recv, h_send, h_recv, o_send, o_recv, g_send, g_recv, own_sem,
):
    n, f, _ = around()
    n_feat, rows, span = zin.shape
    channels, inputs = wt_ref.shape
    hidden = n_feat * channels
    link = Sender()
    ahead = [lax.rem(f + d, n_feat) for d in range(n_feat)]
    behind = [lax.rem(f - d + n_feat, n_feat) for d in range(n_feat)]
    partners = range(1, n_feat)

    wst[0] = wt_ref[...].astype(F32)
    wst[1] = jnp.broadcast_to(bias_ref[...], (inputs, channels)).T
    own_cot = pltpu.make_async_copy(cot_ref.at[:, lanes(f, span)], cin.at[f], own_sem.at[0])
    own_cot.start()
    win[f] = wst[...]
    zin[f] = z_ref[:, lanes(f, span)]
    greet([(n, p) for p in ahead[1:]])
    for d in partners:
        p = ahead[d]
        link.push(z_ref.at[:, lanes(p, span)], zin.at[f], z_send.at[d], z_recv.at[d], n, p)
    for d in partners:
        link.push(wst, win.at[f], w_send.at[d], w_recv.at[d], n, ahead[d])
    for d in partners:
        p = ahead[d]
        link.push(cot_ref.at[:, lanes(p, span)], cin.at[f], c_send.at[d], c_recv.at[d], n, p)
    for d in partners:
        p = behind[d]
        link.arrived(zin.at[p], z_send.at[d], z_recv.at[d])
        link.arrived(win.at[p], w_send.at[d], w_recv.at[d])
    z = zin[...].astype(F32).reshape(n_feat * rows, span).astype(BF16)
    wt = win[:, 0].reshape(hidden, inputs).astype(BF16)
    bias = win[:, 1].reshape(hidden, inputs)[:, :1]
    pre = jnp.dot(wt, z, preferred_element_type=F32) + bias
    for d in partners:
        link.arrived(cin.at[behind[d]], c_send.at[d], c_recv.at[d])
    own_cot.wait()
    s = jax.nn.sigmoid(pre)
    cot = cin[...].reshape(hidden, span).astype(F32)
    g = (cot * s * (1.0 + pre * (1.0 - s))).astype(BF16)
    h = lax.dot_general(wt, g, (((0,), (0,)), ((), ())), preferred_element_type=F32)
    hst[...] = h.reshape(n_feat, rows, span).astype(BF16)
    for d in partners:
        p = ahead[d]
        link.push(hst.at[p], h_ref.at[:, lanes(f, span)], h_send.at[d], h_recv.at[d], n, p)
    own_h = pltpu.make_async_copy(hst.at[f], h_ref.at[:, lanes(f, span)], own_sem.at[1])
    own_h.start()
    gst[:, 0] = (
        lax.dot_general(g, z, (((1,), (1,)), ((), ())), preferred_element_type=F32) * norm
    ).reshape(n_feat, channels, inputs)
    wide = g.astype(F32)
    gb = wide[:, :TILE]
    for t in range(1, span // TILE):
        gb = gb + wide[:, t * TILE:(t + 1) * TILE]
    gst[:, 1] = jnp.broadcast_to(
        jnp.sum(gb, axis=1, keepdims=True) * norm, (hidden, inputs)
    ).reshape(n_feat, channels, inputs)
    for d in partners:
        p = ahead[d]
        link.push(gst.at[p], gin.at[f], g_send.at[d], g_recv.at[d], n, p)
    gin[f] = gst[f]
    ost[...] = (pre * s).astype(BF16).reshape(n_feat, channels, span)
    for d in partners:
        p = ahead[d]
        link.push(ost.at[p], out_ref.at[:, lanes(f, span)], o_send.at[d], o_recv.at[d], n, p)
    own_out = pltpu.make_async_copy(ost.at[f], out_ref.at[:, lanes(f, span)], own_sem.at[2])
    own_out.start()
    for d in partners:
        link.arrived(gin.at[behind[d]], g_send.at[d], g_recv.at[d])
    gw_ref[...] = jnp.sum(gin[...], axis=0)
    for d in partners:
        p = behind[d]
        link.arrived(h_ref.at[:, lanes(p, span)], h_send.at[d], h_recv.at[d])
        link.arrived(out_ref.at[:, lanes(p, span)], o_send.at[d], o_recv.at[d])
    own_h.wait()
    own_out.wait()
    link.finish()


def backward_kernel(
    count, rows, cols, h_ref, tiles_ref, made_out,
    part_ref, own_ref, out_ref, tiles, acc, sems, out_sem,
):
    n = lax.axis_index("node")
    n_node = tiles.shape[0]
    tile_count = acc.shape[0]
    chunks, copy = tile_stream(count, tiles_ref, tiles, sems)

    @pl.loop(1, n_node + 1)
    def _(s):
        j = lax.rem(n + s, n_node)

        @pl.loop(0, chunks(j))
        def _(c):
            copy(j, c).start()

    moved = pltpu.make_async_copy(made_out, out_ref, out_sem)
    moved.start()

    def spread(j):
        @pl.loop(0, chunks(j))
        def _(c):
            copy(j, c).wait()
            made = products(
                count, rows, tiles, lambda t: h_ref[:, lanes(t, TILE)], j, c, ((1,), (0,))
            )
            for u in range(GROUP):
                t = cols[0, j, c * GROUP + u]
                acc[t] = acc[t] + made[u]

    @pl.loop(1, n_node)
    def _(s):
        j = lax.rem(n + s, n_node)
        acc[...] = jnp.zeros_like(acc)
        spread(j)
        for t in range(tile_count):
            part_ref[j, :, t * TILE:(t + 1) * TILE] = acc[t].astype(BF16)

    for t in range(tile_count):
        acc[t] = h_ref[:, t * TILE:(t + 1) * TILE].astype(F32)
    spread(n)
    for t in range(tile_count):
        own_ref[:, t * TILE:(t + 1) * TILE] = acc[t]
    part_ref[n] = jnp.zeros(part_ref.shape[1:], BF16)
    moved.wait()


def reduce_kernel(
    part_ref, own_ref, gw_ref,
    gf_ref, gw_out, gb_out,
    far_in, dl_in, dr_in, hl_in, hr_in, fl_in, fr_in, fy_in,
    far_out, y_out, r_out, l_out, gy, gx, gsum,
    send, recv, g_send, g_recv,
):
    n, f, at = around()
    half = part_ref.shape[2] // 2
    right, left, other, far = at(1, 0), at(-1, 0), at(0, 1), at(2, 0)
    place = lax.rem(n, gx.shape[0])
    link = Sender()
    greet([(right, f), (left, f), (other, f), (far, f)])

    def push(src, dst, k, to):
        link.push(src, dst, send.at[k], recv.at[k], to, f)

    def arrived(dst, k):
        link.arrived(dst, send.at[k], recv.at[k])

    def add(*terms):
        total = terms[0].astype(F32)
        for term in terms[1:]:
            total = total + term.astype(F32)
        return total

    low, high = pl.ds(0, half), pl.ds(half, half)
    push(part_ref.at[at(2, 1)], far_in, 0, other)
    push(part_ref.at[at(1, 1)], dl_in, 1, right)
    push(part_ref.at[at(-1, 1)], dr_in, 2, left)
    link.push(gw_ref, gy, g_send.at[0], g_recv.at[0], other, f)

    arrived(far_in, 0)
    far_out[...] = add(part_ref[far], far_in[...]).astype(BF16)
    push(far_out.at[:, low], hl_in, 3, right)
    push(far_out.at[:, high], hr_in, 4, left)
    arrived(dl_in, 1)
    arrived(dr_in, 2)
    y_out[...] = add(part_ref[other], dl_in[...], dr_in[...]).astype(BF16)
    push(y_out, fy_in, 5, other)
    link.arrived(gy, g_send.at[0], g_recv.at[0])
    gsum[...] = gw_ref[...] + gy[...]
    link.push(gsum, gx.at[place], g_send.at[1], g_recv.at[1], right, f)
    link.push(gsum, gx.at[place], g_send.at[2], g_recv.at[2], left, f)
    link.push(gsum, gx.at[place], g_send.at[3], g_recv.at[3], far, f)
    gx[place] = gsum[...]
    arrived(hl_in, 3)
    r_out[:, low] = add(part_ref[right, :, low], hl_in[...]).astype(BF16)
    r_out[:, high] = part_ref[right, :, high]
    push(r_out, fl_in, 6, right)
    arrived(hr_in, 4)
    l_out[:, low] = part_ref[left, :, low]
    l_out[:, high] = add(part_ref[left, :, high], hr_in[...]).astype(BF16)
    push(l_out, fr_in, 7, left)
    nx = gx.shape[0]
    for k, m in ((1, left), (2, right), (3, far)):
        link.arrived(gx.at[lax.rem(m, nx)], g_send.at[k], g_recv.at[k])
    total = jnp.sum(gx[...], axis=0)
    gw_out[...] = total[0]
    gb_out[...] = total[1].T[:1]
    arrived(fy_in, 5)
    arrived(fl_in, 6)
    arrived(fr_in, 7)
    gf_ref[...] = add(own_ref[...], fl_in[...], fr_in[...], fy_in[...]).astype(BF16)
    link.finish()


def local(features, weight, bias, tile_values, tile_rows, tile_cols, tile_count, cotangent):
    n_node, n_feat = lax.axis_size("node"), lax.axis_size("feat")
    rows, nodes = features.shape
    inputs, channels = weight.shape
    row_tiles = nodes // TILE
    span = row_tiles // n_feat * TILE
    slots = tile_rows.shape[2]
    dma = pltpu.SemaphoreType.DMA
    in_vmem = pl.BlockSpec(memory_space=VMEM)
    in_smem = pl.BlockSpec(memory_space=pltpu.SMEM)
    in_hbm = pl.BlockSpec(memory_space=pltpu.HBM)
    anywhere = pl.BlockSpec(memory_space=pl.ANY)
    shape = jax.ShapeDtypeStruct
    tiles = tile_values[0]

    x_all = pl.pallas_call(
        gather_kernel,
        out_shape=shape((n_node, rows, nodes), BF16),
        in_specs=[in_hbm],
        out_specs=anywhere,
        scratch_shapes=[dma(()), dma((9,)), dma((9,))],
        compiler_params=pltpu.CompilerParams(
            collective_id=0, has_side_effects=True, vmem_limit_bytes=4 << 20
        ),
        name="gather",
    )(features)

    stream = [
        VMEM((n_node, slots, TILE, TILE), BF16),
        VMEM((row_tiles, rows, TILE), F32),
        dma((n_node, slots // GROUP)),
    ]
    z = pl.pallas_call(
        forward_kernel,
        out_shape=shape((rows, nodes), BF16),
        in_specs=[in_smem] * 3 + [in_vmem, in_hbm],
        out_specs=in_vmem,
        scratch_shapes=stream,
        compiler_params=pltpu.CompilerParams(vmem_limit_bytes=24 << 20),
        name="forward",
    )(tile_count, tile_rows, tile_cols, x_all, tiles)

    h, out, gw = pl.pallas_call(
        functools.partial(dense_kernel, 1.0 / float(nodes * n_node) ** 0.5),
        out_shape=(
            shape((rows, nodes), BF16),
            shape((channels, nodes), BF16),
            shape((2, channels, inputs), F32),
        ),
        in_specs=[in_vmem, in_hbm, in_vmem, in_vmem],
        out_specs=(anywhere, anywhere, in_vmem),
        scratch_shapes=[
            VMEM((n_feat, rows, span), BF16),
            VMEM((n_feat, channels, span), BF16),
            VMEM((n_feat, 2, channels, inputs), F32),
            VMEM((2, channels, inputs), F32),
            VMEM((n_feat, rows, span), BF16),
            VMEM((n_feat, channels, span), BF16),
            VMEM((n_feat, 2, channels, inputs), F32),
            VMEM((n_feat, 2, channels, inputs), F32),
        ] + [dma((n_feat,))] * 12 + [dma((3,))],
        compiler_params=pltpu.CompilerParams(
            collective_id=1, has_side_effects=True, vmem_limit_bytes=24 << 20
        ),
        name="dense",
    )(z, cotangent, weight.T, bias.reshape(1, channels))

    part, own, out = pl.pallas_call(
        backward_kernel,
        out_shape=(
            shape((n_node, rows, nodes), BF16),
            shape((rows, nodes), F32),
            shape((channels, nodes), BF16),
        ),
        in_specs=[in_smem] * 3 + [in_vmem, in_hbm, anywhere],
        out_specs=(in_vmem, in_vmem, in_hbm),
        scratch_shapes=stream + [dma(())],
        compiler_params=pltpu.CompilerParams(vmem_limit_bytes=24 << 20),
        name="backward",
    )(tile_count, tile_rows, tile_cols, h, tiles, out)

    block, half = VMEM((rows, nodes), BF16), VMEM((rows, nodes // 2), BF16)
    pair = (2, channels, inputs)
    gf, gwt, gb = pl.pallas_call(
        reduce_kernel,
        out_shape=(
            shape((rows, nodes), BF16),
            shape((channels, inputs), F32),
            shape((1, channels), F32),
        ),
        in_specs=[in_vmem] * 3,
        out_specs=(in_vmem,) * 3,
        scratch_shapes=[block] * 3 + [half] * 2 + [block] * 7 + [
            VMEM(pair, F32), VMEM((n_node // 2,) + pair, F32), VMEM(pair, F32),
            dma((8,)), dma((8,)), dma((4,)), dma((4,)),
        ],
        compiler_params=pltpu.CompilerParams(
            collective_id=2, has_side_effects=True, vmem_limit_bytes=16 << 20
        ),
        name="reduce",
    )(part, own, gw)
    return out, gf, gwt.T, gb.reshape(channels)


def solution(mesh):
    return jax.shard_map(
        local,
        mesh=mesh,
        in_specs=(
            P("feat", "node"),
            P(None, "feat"),
            P("feat"),
            P("node", None, None, None, None),
            P("node", None, None),
            P("node", None, None),
            P("node", None),
            P("feat", "node"),
        ),
        out_specs=(P("feat", "node"), P("feat", "node"), P(None, "feat"), P("feat")),
        check_vma=False,
    )
```

```python
import functools

import jax
import jax.numpy as jnp
from jax import lax
from jax.experimental import pallas as pl
from jax.experimental.pallas import tpu as pltpu
from jax.sharding import PartitionSpec as P

MESH = pl.DeviceIdType.MESH
VMEM = pltpu.VMEM
BF16 = jnp.bfloat16
F32 = jnp.float32
TILE = 128
GROUP = 8


def around():
    n, f = lax.axis_index("node"), lax.axis_index("feat")
    nx = lax.axis_size("node") // 2
    x, y = lax.rem(n, nx), n // nx

    def at(dx, dy):
        return (lax.rem(y + dy, 2)) * nx + lax.rem(x + dx + nx, nx)

    return n, f, at


def remote(src, dst, send, recv, node, feat):
    return pltpu.make_async_remote_copy(
        src_ref=src, dst_ref=dst, send_sem=send, recv_sem=recv, device_id=(node, feat), device_id_type=MESH
    )


def greet(places):
    barrier = pltpu.get_barrier_semaphore()
    for place in places:
        pl.semaphore_signal(barrier, inc=1, device_id=place, device_id_type=MESH)
    pl.semaphore_wait(barrier, len(places))


def lanes(t, width):
    return pl.ds(pl.multiple_of(t * width, width), width)


class Sender:
    def __init__(self):
        self.sent = []

    def push(self, src, dst, send, recv, node, feat):
        self.sent.append(remote(src, dst, send, recv, node, feat))
        self.sent[-1].start()

    def arrived(self, dst, send, recv):
        remote(dst, dst, send, recv, lax.axis_index("node"), lax.axis_index("feat")).wait_recv()

    def finish(self):
        for copy in self.sent:
            copy.wait_send()


def meeting(n, f, at, n_feat):
    other = at(0, 1)
    near = [(at(1, 0), f), (at(-1, 0), f), (other, f)]
    if n_feat != 16:
        return near + [(n, lax.rem(f + d, n_feat)) for d in range(1, n_feat)], []
    z, y, core = f // 4, lax.rem(f // 2, 2), lax.rem(f, 2)
    along_y = [(other, f), (other, z * 4 + (1 - y) * 2 + core)]
    along_z = [(n, lax.rem(z + d, 4) * 4 + y * 2 + core) for d in (1, 3)]
    beside = [(n, f + 1 - 2 * core)]
    return near + along_y[1:] + along_z + beside, [along_y, along_z, along_z, beside]


def relay(rounds, sems, first, last):
    for i in range(first, min(last, len(rounds))):
        for place in rounds[i]:
            pl.semaphore_signal(sems.at[i], inc=1, device_id=place, device_id_type=MESH)
        pl.semaphore_wait(sems.at[i], len(rounds[i]))


def ring(f, n_feat):
    ahead = [lax.rem(f + d, n_feat) for d in range(n_feat)]
    behind = [lax.rem(f - d + n_feat, n_feat) for d in range(n_feat)]
    return ahead, behind, range(1, n_feat)


def split(x):
    high = x.astype(BF16).astype(F32)
    mid = (x - high).astype(BF16).astype(F32)
    lane = lax.broadcasted_iota(jnp.int32, x.shape, 1)
    rest = jnp.where(lane == 1, mid, jnp.where(lane == 2, x - high - mid, 0.0))
    return jnp.where(lane == 0, high, rest).astype(BF16)


def by_tile(x_ref, out_ref):
    for t in range(out_ref.shape[0]):
        out_ref[t] = x_ref[:, t * TILE:(t + 1) * TILE]


def own_products(index, x_ref, tiles, n, out_ref, dims):
    @pl.loop(0, out_ref.shape[0] // GROUP)
    def _(c):
        for u in range(GROUP):
            k = c * GROUP + u
            x = x_ref[index[0, n, k]]
            out_ref[k] = lax.dot_general(x, tiles[n, k], (dims, ((), ())), preferred_element_type=F32)


def gather_kernel(
    x_ref, tiles_ref, cot_ref, count_ref, rows_ref, cols_ref, wt_ref, bias_ref,
    all_ref, tiles, made, cin, win, count_out, rows_out, cols_out,
    x_own, x_tiles, cols, wst, met, local_sem, tile_sem, send, recv, c_send, c_recv, w_send, w_recv,
):
    n, f, at = around()
    n_feat, channels, span = cin.shape
    inputs = wt_ref.shape[1]
    n_node = tiles.shape[0]
    half = x_ref.shape[1] // 2
    right, left, other, far = at(1, 0), at(-1, 0), at(0, 1), at(2, 0)
    ahead, behind, partners = ring(f, n_feat)
    link = Sender()
    here = [
        pltpu.make_async_copy(x_ref, x_own, local_sem.at[0]),
        pltpu.make_async_copy(cols_ref, cols, local_sem.at[1]),
        pltpu.make_async_copy(x_ref, all_ref.at[n], local_sem.at[2]),
        pltpu.make_async_copy(cot_ref.at[:, lanes(f, span)], cin.at[f], local_sem.at[3]),
        pltpu.make_async_copy(count_ref, count_out, local_sem.at[4]),
        pltpu.make_async_copy(rows_ref, rows_out, local_sem.at[5]),
        pltpu.make_async_copy(cols_ref, cols_out, local_sem.at[6]),
    ]
    places, rounds = meeting(n, f, at, n_feat)
    greet(places)

    def whole(m):
        return all_ref.at[m]

    def first(m):
        return all_ref.at[m, :, pl.ds(0, half)]

    def second(m):
        return all_ref.at[m, :, pl.ds(half, half)]

    def push(block, k, to, src=None):
        link.push(block if src is None else src, block, send.at[k], recv.at[k], to, f)

    def arrived(block, k):
        link.arrived(block, send.at[k], recv.at[k])

    push(whole(n), 0, right, x_ref)
    push(whole(n), 1, left, x_ref)
    push(whole(n), 2, other, x_ref)
    for copy in here:
        copy.start()
    moved = [
        pltpu.make_async_copy(tiles_ref.at[j], tiles.at[j], tile_sem.at[s])
        for s, j in enumerate([n] + [lax.rem(n + s, n_node) for s in range(1, n_node)])
    ]
    for copy in moved:
        copy.start()
    wst[0] = wt_ref[...]
    bias = jnp.broadcast_to(bias_ref[...], (inputs, channels)).T
    wst[1] = split(bias)
    win[f] = wst[...]
    relay(rounds, met, 0, 3)
    arrived(whole(left), 0)
    push(first(left), 3, right)
    arrived(whole(right), 1)
    push(second(right), 4, left)
    arrived(whole(other), 2)
    push(whole(other), 5, right)
    push(whole(other), 6, left)
    relay(rounds, met, 3, 4)
    for d in partners:
        p = ahead[d]
        link.push(cot_ref.at[:, lanes(p, span)], cin.at[f], c_send.at[d], c_recv.at[d], n, p)
        link.push(wst, win.at[f], w_send.at[d], w_recv.at[d], n, p)
    here[0].wait()
    here[1].wait()
    moved[0].wait()
    by_tile(x_own, x_tiles)
    own_products(cols, x_tiles, tiles, n, made, ((1,), (1,)))
    arrived(first(far), 3)
    push(first(far), 7, other)
    arrived(second(far), 4)
    push(second(far), 8, other)
    arrived(whole(at(-1, 1)), 5)
    arrived(whole(at(1, 1)), 6)
    for d in partners:
        p = behind[d]
        link.arrived(cin.at[p], c_send.at[d], c_recv.at[d])
        link.arrived(win.at[p], w_send.at[d], w_recv.at[d])
    for copy in here[2:] + moved[1:]:
        copy.wait()
    arrived(first(at(2, 1)), 7)
    arrived(second(at(2, 1)), 8)
    link.finish()


def add_products(count, index, target, tiles, source, acc, j, dims):
    @pl.loop(0, (count[0, j] + (GROUP - 1)) // GROUP)
    def _(c):
        made = []
        for u in range(GROUP):
            k = c * GROUP + u
            x = source(index[0, j, k])
            x = jnp.where(k < count[0, j], x, jnp.zeros_like(x))
            made.append(lax.dot_general(x, tiles[j, k], (dims, ((), ())), preferred_element_type=F32))
        for u in range(GROUP):
            t = target[0, j, c * GROUP + u]
            acc[t] = acc[t] + made[u]


def place_products(target, made, acc, n):
    @pl.loop(0, made.shape[0] // GROUP)
    def _(c):
        for u in range(GROUP):
            t = target[0, n, c * GROUP + u]
            acc[t] = acc[t] + made[c * GROUP + u]


def forward_kernel(count, rows, cols, x_ref, tiles, made, z_ref, acc):
    n = lax.axis_index("node")
    n_node = tiles.shape[0]
    for t in range(acc.shape[0]):
        acc[t] = x_ref[n, :, t * TILE:(t + 1) * TILE].astype(F32)
    place_products(rows, made, acc, n)

    @pl.loop(1, n_node)
    def _(s):
        j = lax.rem(n + s, n_node)
        add_products(
            count, cols, rows, tiles, lambda t: x_ref[j, :, lanes(t, TILE)], acc, j, ((1,), (1,))
        )

    for t in range(acc.shape[0]):
        z_ref[:, t * TILE:(t + 1) * TILE] = acc[t].astype(BF16)


def dense_kernel(
    norm, z_ref, cin, win,
    h_ref, ost, gw_ref,
    zin, hst, gst, gin,
    z_send, z_recv, h_send, h_recv, g_send, g_recv, own_sem,
):
    n, f, _ = around()
    n_feat, rows, span = zin.shape
    channels, inputs = win.shape[2:]
    hidden = n_feat * channels
    link = Sender()
    ahead, behind, partners = ring(f, n_feat)

    zin[f] = z_ref[:, lanes(f, span)]
    greet([(n, p) for p in ahead[1:]])
    for d in partners:
        p = ahead[d]
        link.push(z_ref.at[:, lanes(p, span)], zin.at[f], z_send.at[d], z_recv.at[d], n, p)
    wt = win[:, 0].reshape(hidden, inputs)
    bias = jnp.sum(win[:, 1].reshape(hidden, inputs).astype(F32), axis=1, keepdims=True)
    cot = cin[...].reshape(hidden, span)
    for d in partners:
        link.arrived(zin.at[behind[d]], z_send.at[d], z_recv.at[d])
    z = zin[...].astype(F32).reshape(n_feat * rows, span).astype(BF16)
    pre = jnp.dot(wt, z, preferred_element_type=F32) + bias
    s = jax.nn.sigmoid(pre)
    g = (cot.astype(F32) * s * (1.0 + pre * (1.0 - s))).astype(BF16)
    h = lax.dot_general(wt, g, (((0,), (0,)), ((), ())), preferred_element_type=F32)
    hst[...] = h.reshape(n_feat, rows, span).astype(BF16)
    for d in partners:
        p = ahead[d]
        link.push(hst.at[p], h_ref.at[:, lanes(f, span)], h_send.at[d], h_recv.at[d], n, p)
    own_h = pltpu.make_async_copy(hst.at[f], h_ref.at[:, lanes(f, span)], own_sem)
    own_h.start()
    gst[:, 0] = (
        lax.dot_general(g, z, (((1,), (1,)), ((), ())), preferred_element_type=F32) * norm
    ).astype(BF16).reshape(n_feat, channels, inputs)
    wide = g.astype(F32)
    gb = wide[:, :TILE]
    for t in range(1, span // TILE):
        gb = gb + wide[:, t * TILE:(t + 1) * TILE]
    gb = jnp.sum(gb, axis=1, keepdims=True) * norm
    gst[:, 1] = split(jnp.broadcast_to(gb, (hidden, inputs))).reshape(n_feat, channels, inputs)
    for d in partners:
        p = ahead[d]
        link.push(gst.at[p], gin.at[f], g_send.at[d], g_recv.at[d], n, p)
    gin[f] = gst[f]
    ost[...] = (pre * s).astype(BF16).reshape(n_feat, channels, span)
    for d in partners:
        p = behind[d]
        link.arrived(h_ref.at[:, lanes(p, span)], h_send.at[d], h_recv.at[d])
        link.arrived(gin.at[p], g_send.at[d], g_recv.at[d])
    own_h.wait()
    gw_ref[...] = jnp.sum(gin[...].astype(F32), axis=0)
    link.finish()


def backward_kernel(count, rows, cols, h_ref, tiles, part_ref, acc):
    n = lax.axis_index("node")
    n_node = tiles.shape[0]

    @pl.loop(1, n_node)
    def _(s):
        j = lax.rem(n + s, n_node)
        acc[...] = jnp.zeros_like(acc)
        add_products(count, rows, cols, tiles, lambda t: h_ref[:, lanes(t, TILE)], acc, j, ((1,), (0,)))
        for t in range(acc.shape[0]):
            part_ref[j, :, t * TILE:(t + 1) * TILE] = acc[t].astype(BF16)

    part_ref[n] = jnp.zeros(part_ref.shape[1:], BF16)


def reduce_kernel(
    rows, part_ref, h_ref, tiles, gw_ref, ost,
    fl_in, fr_in, fy_in, made, gw_out, gb_out, out_ref,
    far_in, dl_in, dr_in, hl_in, hr_in, far_out, y_out, r_out, l_out, gy, gx, gsum, h_tiles,
    met, send, recv, g_send, g_recv, o_send, o_recv, own_sem,
):
    n, f, at = around()
    n_feat, _, span = ost.shape
    half = part_ref.shape[2] // 2
    right, left, other, far = at(1, 0), at(-1, 0), at(0, 1), at(2, 0)
    nx = gx.shape[0]
    place = lax.rem(n, nx)
    ahead, behind, partners = ring(f, n_feat)
    link = Sender()
    places, rounds = meeting(n, f, at, n_feat)
    greet(places)

    def push(src, dst, k, to):
        link.push(src, dst, send.at[k], recv.at[k], to, f)

    def arrived(dst, k):
        link.arrived(dst, send.at[k], recv.at[k])

    def add(*terms):
        total = terms[0].astype(F32)
        for term in terms[1:]:
            total = total + term.astype(F32)
        return total

    low, high = pl.ds(0, half), pl.ds(half, half)
    push(part_ref.at[at(2, 1)], far_in, 0, other)
    push(part_ref.at[at(1, 1)], dl_in, 1, right)
    push(part_ref.at[at(-1, 1)], dr_in, 2, left)
    link.push(gw_ref, gy, g_send.at[0], g_recv.at[0], other, f)
    own_out = pltpu.make_async_copy(ost.at[f], out_ref.at[:, lanes(f, span)], own_sem)
    own_out.start()
    relay(rounds, met, 0, 3)

    arrived(far_in, 0)
    far_out[...] = add(part_ref[far], far_in[...]).astype(BF16)
    push(far_out.at[:, low], hl_in, 3, right)
    push(far_out.at[:, high], hr_in, 4, left)
    arrived(dl_in, 1)
    arrived(dr_in, 2)
    y_out[...] = add(part_ref[other], dl_in[...], dr_in[...]).astype(BF16)
    push(y_out, fy_in, 5, other)
    link.arrived(gy, g_send.at[0], g_recv.at[0])
    gsum[...] = gw_ref[...] + gy[...]
    link.push(gsum, gx.at[place], g_send.at[1], g_recv.at[1], right, f)
    link.push(gsum, gx.at[place], g_send.at[2], g_recv.at[2], left, f)
    gx[place] = gsum[...]
    arrived(hl_in, 3)
    r_out[:, low] = add(part_ref[right, :, low], hl_in[...]).astype(BF16)
    r_out[:, high] = part_ref[right, :, high]
    push(r_out, fl_in, 6, right)
    arrived(hr_in, 4)
    l_out[:, low] = part_ref[left, :, low]
    l_out[:, high] = add(part_ref[left, :, high], hr_in[...]).astype(BF16)
    push(l_out, fr_in, 7, left)
    link.push(gsum, gx.at[place], g_send.at[3], g_recv.at[3], far, f)
    relay(rounds, met, 3, 4)
    for d in partners:
        p = ahead[d]
        link.push(ost.at[p], out_ref.at[:, lanes(f, span)], o_send.at[d], o_recv.at[d], n, p)
    by_tile(h_ref, h_tiles)
    own_products(rows, h_tiles, tiles, n, made, ((1,), (0,)))
    for k, m in ((1, left), (2, right), (3, far)):
        link.arrived(gx.at[lax.rem(m, nx)], g_send.at[k], g_recv.at[k])
    total = jnp.sum(gx[...], axis=0)
    gw_out[...] = total[0]
    gb_out[...] = jnp.sum(total[1].T, axis=0, keepdims=True)
    arrived(fy_in, 5)
    arrived(fl_in, 6)
    arrived(fr_in, 7)
    for d in partners:
        link.arrived(out_ref.at[:, lanes(behind[d], span)], o_send.at[d], o_recv.at[d])
    own_out.wait()
    link.finish()


def final_kernel(
    cols, h_ref, fl, fr, fy, made, gw_ref, gb_ref, made_out,
    gf_ref, gw_out, gb_out, out_ref, acc, out_sem,
):
    n = lax.axis_index("node")
    moved = pltpu.make_async_copy(made_out, out_ref, out_sem)
    moved.start()
    for t in range(acc.shape[0]):
        span = slice(t * TILE, (t + 1) * TILE)
        acc[t] = (
            h_ref[:, span].astype(F32) + fl[:, span].astype(F32)
            + fr[:, span].astype(F32) + fy[:, span].astype(F32)
        )
    place_products(cols, made, acc, n)
    for t in range(acc.shape[0]):
        gf_ref[:, t * TILE:(t + 1) * TILE] = acc[t].astype(BF16)
    gw_out[...] = gw_ref[...]
    gb_out[...] = gb_ref[...]
    moved.wait()


def local(features, weight, bias, tile_values, tile_rows, tile_cols, tile_count, cotangent):
    n_node, n_feat = lax.axis_size("node"), lax.axis_size("feat")
    rows, nodes = features.shape
    inputs, channels = weight.shape
    row_tiles = nodes // TILE
    span = row_tiles // n_feat * TILE
    slots = tile_rows.shape[2]
    dma = pltpu.SemaphoreType.DMA
    in_vmem = pl.BlockSpec(memory_space=VMEM)
    in_smem = pl.BlockSpec(memory_space=pltpu.SMEM)
    in_hbm = pl.BlockSpec(memory_space=pltpu.HBM)
    shape = jax.ShapeDtypeStruct
    block = (rows, nodes)
    pair = (2, channels, inputs)

    def params(mib, **more):
        return pltpu.CompilerParams(vmem_limit_bytes=mib << 20, **more)

    def keep(x):
        return pltpu.with_memory_space_constraint(x, pltpu.HBM)

    def pairs(k):
        return [dma((n_feat,))] * k

    met = pltpu.SemaphoreType.REGULAR((4,))
    x_all, tiles, made, cin, win, count, row_list, col_list = pl.pallas_call(
        gather_kernel,
        out_shape=(
            shape((n_node,) + block, BF16),
            shape(tile_values.shape[1:], BF16),
            shape((slots, rows, TILE), F32),
            shape((n_feat, channels, span), BF16),
            shape((n_feat,) + pair, BF16),
            shape(tile_count.shape, jnp.int32),
            shape(tile_rows.shape, jnp.int32),
            shape(tile_cols.shape, jnp.int32),
        ),
        in_specs=[in_hbm] * 6 + [in_vmem] * 2,
        out_specs=(in_vmem,) * 8,
        scratch_shapes=[
            VMEM(block, BF16), VMEM((row_tiles, rows, TILE), BF16), pltpu.SMEM(tile_cols.shape, jnp.int32), VMEM(pair, BF16),
            met, dma((7,)), dma((n_node,)), dma((9,)), dma((9,)),
        ] + pairs(4),
        compiler_params=params(20, collective_id=0, has_side_effects=True),
        name="gather",
    )(
        keep(features), keep(tile_values[0]), keep(cotangent),
        keep(tile_count), keep(tile_rows), keep(tile_cols),
        weight.T, bias.reshape(1, channels),
    )

    acc = VMEM((row_tiles, rows, TILE), F32)
    z = pl.pallas_call(
        forward_kernel,
        out_shape=shape(block, BF16),
        in_specs=[in_smem] * 3 + [in_vmem] * 3,
        out_specs=in_vmem,
        scratch_shapes=[acc],
        compiler_params=params(16),
        name="forward",
    )(count, row_list, col_list, x_all, tiles, made)

    h, ost, gw = pl.pallas_call(
        functools.partial(dense_kernel, 1.0 / float(nodes * n_node) ** 0.5),
        out_shape=(
            shape(block, BF16),
            shape((n_feat, channels, span), BF16),
            shape(pair, F32),
        ),
        in_specs=[in_vmem] * 3,
        out_specs=(in_vmem,) * 3,
        scratch_shapes=[
            VMEM((n_feat, rows, span), BF16),
            VMEM((n_feat, rows, span), BF16),
            VMEM((n_feat,) + pair, BF16),
            VMEM((n_feat,) + pair, BF16),
        ] + pairs(6) + [dma(())],
        compiler_params=params(16, collective_id=1, has_side_effects=True),
        name="dense",
    )(z, cin, win)

    part = pl.pallas_call(
        backward_kernel,
        out_shape=shape((n_node,) + block, BF16),
        in_specs=[in_smem] * 3 + [in_vmem] * 2,
        out_specs=in_vmem,
        scratch_shapes=[acc],
        compiler_params=params(16),
        name="backward",
    )(count, row_list, col_list, h, tiles)

    whole, half = VMEM(block, BF16), VMEM((rows, nodes // 2), BF16)
    fl, fr, fy, made, gwt, gb, out = pl.pallas_call(
        reduce_kernel,
        out_shape=(
            shape(block, BF16),
            shape(block, BF16),
            shape(block, BF16),
            shape((slots, rows, TILE), F32),
            shape((channels, inputs), F32),
            shape((1, channels), F32),
            shape((channels, nodes), BF16),
        ),
        in_specs=[in_smem] + [in_vmem] * 5,
        out_specs=(in_vmem,) * 7,
        scratch_shapes=[whole] * 3 + [half] * 2 + [whole] * 4 + [
            VMEM(pair, F32), VMEM((n_node // 2,) + pair, F32), VMEM(pair, F32),
            VMEM((row_tiles, rows, TILE), BF16),
            met, dma((8,)), dma((8,)), dma((4,)), dma((4,)),
        ] + pairs(2) + [dma(())],
        compiler_params=params(16, collective_id=2, has_side_effects=True),
        name="reduce",
    )(row_list, part, h, tiles, gw, ost)

    gf, gwt, gb, out = pl.pallas_call(
        final_kernel,
        out_shape=(
            shape(block, BF16),
            shape((channels, inputs), F32),
            shape((1, channels), F32),
            shape((channels, nodes), BF16),
        ),
        in_specs=[in_smem] + [in_vmem] * 8,
        out_specs=(in_vmem,) * 3 + (in_hbm,),
        scratch_shapes=[acc, dma(())],
        compiler_params=params(16),
        name="final",
    )(col_list, h, fl, fr, fy, made, gwt, gb, out)
    return out, gf, gwt.T, gb.reshape(channels)


def solution(mesh):
    return jax.shard_map(
        local,
        mesh=mesh,
        in_specs=(
            P("feat", "node"),
            P(None, "feat"),
            P("feat"),
            P("node", None, None, None, None),
            P("node", None, None),
            P("node", None, None),
            P("node", None),
            P("feat", "node"),
        ),
        out_specs=(P("feat", "node"), P("feat", "node"), P(None, "feat"), P("feat")),
        check_vma=False,
    )
```

```python
import functools

import jax
import jax.numpy as jnp
from jax import lax
from jax.experimental import pallas as pl
from jax.experimental.pallas import tpu as pltpu
from jax.sharding import PartitionSpec as P

MESH = pl.DeviceIdType.MESH
VMEM = pltpu.VMEM
BF16 = jnp.bfloat16
F32 = jnp.float32
TILE = 128
GROUP = 8
LONG = 16


def around():
    n, f = lax.axis_index("node"), lax.axis_index("feat")
    nx = lax.axis_size("node") // 2
    x, y = lax.rem(n, nx), n // nx

    def at(dx, dy):
        return (lax.rem(y + dy, 2)) * nx + lax.rem(x + dx + nx, nx)

    return n, f, at


def remote(src, dst, send, recv, node, feat):
    return pltpu.make_async_remote_copy(
        src_ref=src, dst_ref=dst, send_sem=send, recv_sem=recv, device_id=(node, feat), device_id_type=MESH
    )


def greet(places):
    barrier = pltpu.get_barrier_semaphore()
    for place in places:
        pl.semaphore_signal(barrier, inc=1, device_id=place, device_id_type=MESH)


def met(places):
    pl.semaphore_wait(pltpu.get_barrier_semaphore(), len(places))


def lanes(t, width):
    return pl.ds(pl.multiple_of(t * width, width), width)


class Sender:
    def __init__(self):
        self.sent = []

    def push(self, src, dst, send, recv, node, feat):
        self.sent.append(remote(src, dst, send, recv, node, feat))
        self.sent[-1].start()

    def arrived(self, dst, send, recv):
        remote(dst, dst, send, recv, lax.axis_index("node"), lax.axis_index("feat")).wait_recv()

    def finish(self):
        for copy in self.sent:
            copy.wait_send()


def ring(f, n_feat):
    if n_feat != 16:
        return [(d, lax.rem(f + d, n_feat), lax.rem(f - d + n_feat, n_feat)) for d in range(1, n_feat)]
    z, y, core = f // 4, lax.rem(f // 2, 2), lax.rem(f, 2)

    def by(dz, dy, dc):
        return lax.rem(z + dz + 4, 4) * 4 + lax.rem(y + dy, 2) * 2 + lax.rem(core + dc, 2)

    offsets = [(dz, dy, dc) for dz in (2, 1, 3, 0) for dy in (1, 0) for dc in (1, 0)][:-1]
    offsets.sort(key=lambda d: -(min(d[0], 4 - d[0]) + 2 * d[1] + d[2]))
    return [(dz * 4 + dy * 2 + dc, by(dz, dy, dc), by(-dz, dy, dc)) for dz, dy, dc in offsets]


def everyone(n, f, at, partners):
    near = [(at(1, 0), f), (at(-1, 0), f), (at(0, 1), f)]
    return near + [(n, p) for _, p, _ in partners]


def split(x):
    high = x.astype(BF16).astype(F32)
    mid = (x - high).astype(BF16).astype(F32)
    lane = lax.broadcasted_iota(jnp.int32, x.shape, 1)
    rest = jnp.where(lane == 1, mid, jnp.where(lane == 2, x - high - mid, 0.0))
    return jnp.where(lane == 0, high, rest).astype(BF16)


def by_tile(x_ref, out_ref):
    for t in range(out_ref.shape[0]):
        out_ref[t] = x_ref[:, t * TILE:(t + 1) * TILE]


def own_products(index, x_ref, tiles, n, out_ref, dims):
    @pl.loop(0, out_ref.shape[0] // GROUP)
    def _(c):
        for u in range(GROUP):
            k = c * GROUP + u
            x = x_ref[index(k)]
            out_ref[k] = lax.dot_general(x, tiles[n * out_ref.shape[0] + k], (dims, ((), ())), preferred_element_type=F32)


def slot_list(count, rows, cols, n, n_node, out_ref):
    slots = rows.shape[2]
    width = out_ref.shape[1]
    q = lax.broadcasted_iota(jnp.int32, (slots, width), 1)
    k = lax.broadcasted_iota(jnp.int32, (slots, width), 0)
    line = lax.broadcasted_iota(jnp.int32, (8, slots), 0)
    number = lax.broadcasted_iota(jnp.int32, (8, slots), 1)
    total = jnp.zeros((8, width), F32)
    base = 0
    for s in range(1, n_node):
        j = lax.rem(n + s, n_node)
        used = count[0, j]
        hit = jnp.where((q == k + base) & (k < used), 1.0, 0.0).astype(BF16)
        mine = jnp.where(line == 0, number, jnp.where(line == 1, j, 0))
        mine = jnp.where(line == 2, rows[0, pl.ds(j, 1)], jnp.where(line == 3, cols[0, pl.ds(j, 1)], mine))
        total = total + jnp.dot(mine.astype(F32).astype(BF16), hit, preferred_element_type=F32)
        base = base + used
    out_ref[...] = jnp.where(
        lax.broadcasted_iota(jnp.int32, out_ref.shape, 0) == 6, base, total.astype(jnp.int32)
    )
    out_ref[4:5, :slots] = rows[0, pl.ds(n, 1)]
    out_ref[5:6, :slots] = cols[0, pl.ds(n, 1)]


def gather_kernel(
    x_ref, tiles_ref, cot_ref, count_ref, rows_ref, cols_ref, wt_ref, bias_ref,
    all_ref, tiles, made, cin, win, list_out,
    x_own, x_tiles, count, cols, rows_in, cols_in, wt, bias_in, wst,
    local_sem, tile_sem, send, recv, c_send, c_recv, w_send, w_recv,
):
    n, f, at = around()
    n_feat, channels, span = cin.shape
    inputs = wt_ref.shape[1]
    n_node = count_ref.shape[1]
    slots = made.shape[0]
    half = x_ref.shape[1] // 2
    right, left, other, far = at(1, 0), at(-1, 0), at(0, 1), at(2, 0)
    link = Sender()
    here = [
        pltpu.make_async_copy(src, dst, local_sem.at[i])
        for i, (src, dst) in enumerate([
            (wt_ref, wt), (bias_ref, bias_in), (count_ref, count), (rows_ref, rows_in), (cols_ref, cols_in),
            (cols_ref, cols), (x_ref, x_own),
            (x_ref, all_ref.at[n]), (cot_ref.at[:, lanes(f, span)], cin.at[f]),
        ])
    ]
    moved = [
        pltpu.make_async_copy(
            tiles_ref.at[pl.ds(j * slots, slots)], tiles.at[pl.ds(j * slots, slots)], tile_sem.at[s]
        )
        for s, j in enumerate([n] + [lax.rem(n + s, n_node) for s in range(1, n_node)])
    ]
    partners = ring(f, n_feat)
    places = everyone(n, f, at, partners)
    greet(places)
    for copy in here:
        copy.start()
    met(places)

    low, high = pl.ds(0, half), pl.ds(half, half)

    def push(m, part, k, to, src=None):
        block = all_ref.at[m, :, part]
        link.push(block if src is None else src.at[:, part], block, send.at[k], recv.at[k], to, f)

    def arrived(m, part, k):
        link.arrived(all_ref.at[m, :, part], send.at[k], recv.at[k])

    push(n, low, 0, right, x_ref)
    push(n, high, 1, left, x_ref)
    push(n, low, 2, other, x_ref)
    push(n, high, 3, right, x_ref)
    push(n, low, 4, left, x_ref)
    push(n, high, 5, other, x_ref)
    for d, p, _ in partners:
        link.push(cot_ref.at[:, lanes(p, span)], cin.at[f], c_send.at[d], c_recv.at[d], n, p)
    for copy in here[:2]:
        copy.wait()
    wst[0] = wt[...]
    wst[1] = split(jnp.broadcast_to(bias_in[...], (inputs, channels)).T)
    win[f] = wst[...]
    for d, p, _ in partners:
        link.push(wst, win.at[f], w_send.at[d], w_recv.at[d], n, p)
    for copy in moved:
        copy.start()
    arrived(left, low, 0)
    push(left, low, 6, right)
    arrived(right, high, 1)
    push(right, high, 7, left)
    arrived(other, low, 2)
    push(other, low, 8, right)
    push(other, low, 9, left)
    arrived(other, high, 5)
    push(other, high, 10, right)
    push(other, high, 11, left)
    for copy in here[2:7]:
        copy.wait()
    slot_list(count, rows_in, cols_in, n, n_node, list_out)
    arrived(far, low, 6)
    push(far, low, 12, other)
    arrived(far, high, 7)
    push(far, high, 13, other)
    moved[0].wait()
    by_tile(x_own, x_tiles)
    own_products(lambda k: cols[0, n, k], x_tiles, tiles, n, made, ((1,), (1,)))
    arrived(left, high, 3)
    arrived(right, low, 4)
    for m, k in ((at(-1, 1), 0), (at(1, 1), 1)):
        arrived(m, low, 8 + k)
        arrived(m, high, 10 + k)
    for d, _, p in partners:
        link.arrived(cin.at[p], c_send.at[d], c_recv.at[d])
        link.arrived(win.at[p], w_send.at[d], w_recv.at[d])
    for copy in here[7:] + moved[1:]:
        copy.wait()
    arrived(at(2, 1), low, 12)
    arrived(at(2, 1), high, 13)
    link.finish()


def add_products(slots, listed, tiles, source, target, acc, dims):
    total = listed[6, 0]

    @pl.loop(0, (total + (LONG - 1)) // LONG)
    def _(c):
        made = []
        for u in range(LONG):
            q = c * LONG + u
            k, j = listed[0, q], listed[1, q]
            x = source(j, listed[2, q], listed[3, q])
            x = jnp.where(q < total, x, jnp.zeros_like(x))
            made.append(
                lax.dot_general(x, tiles[j * slots + k], (dims, ((), ())), preferred_element_type=F32)
            )
        for u in range(LONG):
            q = c * LONG + u
            t = target(listed[1, q], listed[2, q], listed[3, q])
            acc[t] = acc[t] + made[u]


def place_products(listed, line, made, acc):
    @pl.loop(0, made.shape[0] // GROUP)
    def _(c):
        for u in range(GROUP):
            t = listed[line, c * GROUP + u]
            acc[t] = acc[t] + made[c * GROUP + u]


def forward_kernel(listed, x_ref, tiles, made, z_ref, acc):
    n = lax.axis_index("node")
    for t in range(acc.shape[0]):
        acc[t] = x_ref[n, :, t * TILE:(t + 1) * TILE].astype(F32)
    place_products(listed, 4, made, acc)
    add_products(
        made.shape[0], listed, tiles,
        lambda j, r, c: x_ref[j, :, lanes(c, TILE)], lambda j, r, c: r, acc, ((1,), (1,)),
    )
    for t in range(acc.shape[0]):
        z_ref[:, t * TILE:(t + 1) * TILE] = acc[t].astype(BF16)


def dense_kernel(
    norm, z_ref, cin, win,
    h_ref, ost, gw_ref,
    zin, hst, gst, gin,
    z_send, z_recv, h_send, h_recv, g_send, g_recv, own_sem,
):
    n, f, _ = around()
    n_feat, rows, span = zin.shape
    channels, inputs = win.shape[2:]
    hidden = n_feat * channels
    link = Sender()
    partners = ring(f, n_feat)
    places = [(n, p) for _, p, _ in partners]
    greet(places)
    zin[f] = z_ref[:, lanes(f, span)]
    met(places)
    for d, p, _ in partners:
        link.push(z_ref.at[:, lanes(p, span)], zin.at[f], z_send.at[d], z_recv.at[d], n, p)
    wt = win[:, 0].reshape(hidden, inputs)
    bias = jnp.sum(win[:, 1].reshape(hidden, inputs).astype(F32), axis=1, keepdims=True)
    cot = cin[...].reshape(hidden, span)
    for d, _, p in partners:
        link.arrived(zin.at[p], z_send.at[d], z_recv.at[d])
    z = zin[...].astype(F32).reshape(n_feat * rows, span).astype(BF16)
    pre = jnp.dot(wt, z, preferred_element_type=F32) + bias
    s = jax.nn.sigmoid(pre)
    g = (cot.astype(F32) * s * (1.0 + pre * (1.0 - s))).astype(BF16)
    h = lax.dot_general(wt, g, (((0,), (0,)), ((), ())), preferred_element_type=F32)
    hst[...] = h.reshape(n_feat, rows, span).astype(BF16)
    for d, p, _ in partners:
        link.push(hst.at[p], h_ref.at[:, lanes(f, span)], h_send.at[d], h_recv.at[d], n, p)
    own_h = pltpu.make_async_copy(hst.at[f], h_ref.at[:, lanes(f, span)], own_sem)
    own_h.start()
    both = jnp.concatenate([z, jnp.ones_like(z)], axis=0)
    sums = lax.dot_general(g, both, (((1,), (1,)), ((), ())), preferred_element_type=F32) * norm
    gst[:, 0] = sums[:, :inputs].astype(BF16).reshape(n_feat, channels, inputs)
    gst[:, 1] = split(sums[:, inputs:]).reshape(n_feat, channels, inputs)
    for d, p, _ in partners:
        link.push(gst.at[p], gin.at[f], g_send.at[d], g_recv.at[d], n, p)
    gin[f] = gst[f]
    ost[...] = (pre * s).astype(BF16).reshape(n_feat, channels, span)
    for d, _, p in partners:
        link.arrived(h_ref.at[:, lanes(p, span)], h_send.at[d], h_recv.at[d])
        link.arrived(gin.at[p], g_send.at[d], g_recv.at[d])
    own_h.wait()
    gw_ref[...] = jnp.sum(gin[...].astype(F32), axis=0)
    link.finish()


def backward_kernel(listed, h_ref, tiles, part_ref, acc):
    n_node = part_ref.shape[0]
    row_tiles = acc.shape[0] // n_node
    acc[...] = jnp.zeros_like(acc)
    add_products(
        tiles.shape[0] // n_node, listed, tiles,
        lambda j, r, c: h_ref[:, lanes(r, TILE)], lambda j, r, c: j * row_tiles + c, acc, ((1,), (0,)),
    )
    for j in range(n_node):
        for t in range(row_tiles):
            part_ref[j, :, t * TILE:(t + 1) * TILE] = acc[j * row_tiles + t].astype(BF16)


def reduce_kernel(
    listed, part_ref, h_ref, tiles, gw_ref, ost,
    fl_in, fr_in, fy_in, made, gw_out, gb_out, out_ref,
    far_in, dl_in, dr_in, hl_in, hr_in, hl_out, hr_out, y_out, r_out, l_out, g_in, g_out, h_tiles,
    send, recv, g_send, g_recv, o_send, o_recv, own_sem,
):
    n, f, at = around()
    n_feat, _, span = ost.shape
    n_node, _, nodes = part_ref.shape
    half = nodes // 2
    right, left, other, far = at(1, 0), at(-1, 0), at(0, 1), at(2, 0)
    x = lax.rem(n, n_node // 2)
    first = at(1 - 2 * lax.rem(x, 2), 0)
    second = at(2 * lax.rem(x, 2) - 1, 0)
    link = Sender()
    partners = ring(f, n_feat)
    places = everyone(n, f, at, partners)
    greet(places)
    met(places)

    def push(src, dst, k, to):
        link.push(src, dst, send.at[k], recv.at[k], to, f)

    def arrived(dst, k):
        link.arrived(dst, send.at[k], recv.at[k])

    def add(*terms):
        total = terms[0].astype(F32)
        for term in terms[1:]:
            total = total + term.astype(F32)
        return total.astype(BF16)

    low, high = pl.ds(0, half), pl.ds(half, half)
    halves = (low, high)
    for i, part in enumerate(halves):
        push(part_ref.at[at(2, 1), :, part], far_in.at[:, part], i, other)
        push(part_ref.at[at(1, 1), :, part], dl_in.at[:, part], 2 + i, right)
        push(part_ref.at[at(-1, 1), :, part], dr_in.at[:, part], 4 + i, left)
    link.push(gw_ref, g_in.at[0], g_send.at[0], g_recv.at[0], first, f)
    own_out = pltpu.make_async_copy(ost.at[f], out_ref.at[:, lanes(f, span)], own_sem)
    own_out.start()
    for d, p, _ in partners:
        link.push(ost.at[p], out_ref.at[:, lanes(f, span)], o_send.at[d], o_recv.at[d], n, p)
    arrived(far_in.at[:, low], 0)
    hl_out[...] = add(part_ref[far, :, low], far_in[:, low])
    push(hl_out, hl_in, 6, right)
    arrived(far_in.at[:, high], 1)
    hr_out[...] = add(part_ref[far, :, high], far_in[:, high])
    push(hr_out, hr_in, 7, left)
    push(part_ref.at[right, :, high], fl_in.at[:, high], 8, right)
    push(part_ref.at[left, :, low], fr_in.at[:, low], 9, left)
    link.arrived(g_in.at[0], g_send.at[0], g_recv.at[0])
    g_out[0] = gw_ref[...] + g_in[0]
    link.push(g_out.at[0], g_in.at[1], g_send.at[1], g_recv.at[1], second, f)
    for i, part in enumerate(halves):
        arrived(dl_in.at[:, part], 2 + i)
        arrived(dr_in.at[:, part], 4 + i)
        y_out[:, part] = add(part_ref[other, :, part], dl_in[:, part], dr_in[:, part])
        push(y_out.at[:, part], fy_in.at[:, part], 10 + i, other)
    link.arrived(g_in.at[1], g_send.at[1], g_recv.at[1])
    g_out[1] = g_out[0] + g_in[1]
    link.push(g_out.at[1], g_in.at[2], g_send.at[2], g_recv.at[2], other, f)
    arrived(hl_in, 6)
    r_out[...] = add(part_ref[right, :, low], hl_in[...])
    push(r_out, fl_in.at[:, low], 12, right)
    arrived(hr_in, 7)
    l_out[...] = add(part_ref[left, :, high], hr_in[...])
    push(l_out, fr_in.at[:, high], 13, left)
    by_tile(h_ref, h_tiles)
    own_products(lambda k: listed[4, k], h_tiles, tiles, n, made, ((1,), (0,)))
    link.arrived(g_in.at[2], g_send.at[2], g_recv.at[2])
    total = g_out[1] + g_in[2]
    gw_out[...] = total[0]
    gb_out[...] = jnp.sum(total[1].T, axis=0, keepdims=True)
    for i, part in enumerate(halves):
        arrived(fy_in.at[:, part], 10 + i)
    arrived(fl_in.at[:, high], 8)
    arrived(fr_in.at[:, low], 9)
    arrived(fl_in.at[:, low], 12)
    arrived(fr_in.at[:, high], 13)
    for d, _, p in partners:
        link.arrived(out_ref.at[:, lanes(p, span)], o_send.at[d], o_recv.at[d])
    own_out.wait()
    link.finish()


def final_kernel(
    listed, h_ref, fl, fr, fy, made, gw_ref, gb_ref, made_out,
    gf_ref, gw_out, gb_out, out_ref, acc, out_sem,
):
    moved = pltpu.make_async_copy(made_out, out_ref, out_sem)
    moved.start()
    for t in range(acc.shape[0]):
        span = slice(t * TILE, (t + 1) * TILE)
        acc[t] = (
            h_ref[:, span].astype(F32) + fl[:, span].astype(F32)
            + fr[:, span].astype(F32) + fy[:, span].astype(F32)
        )
    place_products(listed, 5, made, acc)
    for t in range(acc.shape[0]):
        gf_ref[:, t * TILE:(t + 1) * TILE] = acc[t].astype(BF16)
    gw_out[...] = gw_ref[...]
    gb_out[...] = gb_ref[...]
    moved.wait()


def local(features, weight, bias, tile_values, tile_rows, tile_cols, tile_count, cotangent):
    n_node, n_feat = lax.axis_size("node"), lax.axis_size("feat")
    rows, nodes = features.shape
    inputs, channels = weight.shape
    row_tiles = nodes // TILE
    span = row_tiles // n_feat * TILE
    slots = tile_rows.shape[2]
    dma = pltpu.SemaphoreType.DMA
    in_vmem = pl.BlockSpec(memory_space=VMEM)
    in_smem = pl.BlockSpec(memory_space=pltpu.SMEM)
    in_hbm = pl.BlockSpec(memory_space=pltpu.HBM)
    shape = jax.ShapeDtypeStruct
    block = (rows, nodes)
    pair = (2, channels, inputs)

    def params(mib, **more):
        return pltpu.CompilerParams(vmem_limit_bytes=mib << 20, **more)

    def keep(x):
        return pltpu.with_memory_space_constraint(x, pltpu.HBM)

    def pairs(k):
        return [dma((n_feat,))] * k

    x_all, tiles, made, cin, win, listed = pl.pallas_call(
        gather_kernel,
        out_shape=(
            shape((n_node,) + block, BF16),
            shape((n_node * slots, TILE, TILE), BF16),
            shape((slots, rows, TILE), F32),
            shape((n_feat, channels, span), BF16),
            shape((n_feat,) + pair, BF16),
            shape((8, n_node * slots), jnp.int32),
        ),
        in_specs=[in_hbm] * 8,
        out_specs=(in_vmem,) * 6,
        scratch_shapes=[
            VMEM(block, BF16), VMEM((row_tiles, rows, TILE), BF16),
            pltpu.SMEM(tile_count.shape, jnp.int32), pltpu.SMEM(tile_cols.shape, jnp.int32),
            VMEM(tile_rows.shape, jnp.int32), VMEM(tile_cols.shape, jnp.int32),
            VMEM((channels, inputs), BF16), VMEM((1, channels), F32), VMEM(pair, BF16),
            dma((9,)), dma((n_node,)), dma((14,)), dma((14,)),
        ] + pairs(4),
        compiler_params=params(20, collective_id=0, has_side_effects=True),
        name="gather",
    )(
        keep(features), keep(tile_values.reshape(n_node * slots, TILE, TILE)), keep(cotangent),
        keep(tile_count), keep(tile_rows), keep(tile_cols),
        keep(weight.T), keep(bias.reshape(1, channels)),
    )

    acc = VMEM((row_tiles, rows, TILE), F32)
    z = pl.pallas_call(
        forward_kernel,
        out_shape=shape(block, BF16),
        in_specs=[in_smem] + [in_vmem] * 3,
        out_specs=in_vmem,
        scratch_shapes=[acc],
        compiler_params=params(16),
        name="forward",
    )(listed, x_all, tiles, made)

    h, ost, gw = pl.pallas_call(
        functools.partial(dense_kernel, 1.0 / float(nodes * n_node) ** 0.5),
        out_shape=(
            shape(block, BF16),
            shape((n_feat, channels, span), BF16),
            shape(pair, F32),
        ),
        in_specs=[in_vmem] * 3,
        out_specs=(in_vmem,) * 3,
        scratch_shapes=[
            VMEM((n_feat, rows, span), BF16),
            VMEM((n_feat, rows, span), BF16),
            VMEM((n_feat,) + pair, BF16),
            VMEM((n_feat,) + pair, BF16),
        ] + pairs(6) + [dma(())],
        compiler_params=params(16, collective_id=1, has_side_effects=True),
        name="dense",
    )(z, cin, win)

    part = pl.pallas_call(
        backward_kernel,
        out_shape=shape((n_node,) + block, BF16),
        in_specs=[in_smem] + [in_vmem] * 2,
        out_specs=in_vmem,
        scratch_shapes=[VMEM((n_node * row_tiles, rows, TILE), F32)],
        compiler_params=params(16),
        name="backward",
    )(listed, h, tiles)

    whole, half = VMEM(block, BF16), VMEM((rows, nodes // 2), BF16)
    fl, fr, fy, made, gwt, gb, out = pl.pallas_call(
        reduce_kernel,
        out_shape=(
            shape(block, BF16),
            shape(block, BF16),
            shape(block, BF16),
            shape((slots, rows, TILE), F32),
            shape((channels, inputs), F32),
            shape((1, channels), F32),
            shape((channels, nodes), BF16),
        ),
        in_specs=[in_smem] + [in_vmem] * 5,
        out_specs=(in_vmem,) * 7,
        scratch_shapes=[whole] * 3 + [half] * 4 + [whole] + [half] * 2 + [
            VMEM((3,) + pair, F32), VMEM((2,) + pair, F32),
            VMEM((row_tiles, rows, TILE), BF16),
            dma((14,)), dma((14,)), dma((3,)), dma((3,)),
        ] + pairs(2) + [dma(())],
        compiler_params=params(16, collective_id=2, has_side_effects=True),
        name="reduce",
    )(listed, part, h, tiles, gw, ost)

    gf, gwt, gb, out = pl.pallas_call(
        final_kernel,
        out_shape=(
            shape(block, BF16),
            shape((channels, inputs), F32),
            shape((1, channels), F32),
            shape((channels, nodes), BF16),
        ),
        in_specs=[in_smem] + [in_vmem] * 8,
        out_specs=(in_vmem,) * 3 + (in_hbm,),
        scratch_shapes=[acc, dma(())],
        compiler_params=params(16),
        name="final",
    )(listed, h, fl, fr, fy, made, gwt, gb, out)
    return out, gf, gwt.T, gb.reshape(channels)


def solution(mesh):
    return jax.shard_map(
        local,
        mesh=mesh,
        in_specs=(
            P("feat", "node"),
            P(None, "feat"),
            P("feat"),
            P("node", None, None, None, None),
            P("node", None, None),
            P("node", None, None),
            P("node", None),
            P("feat", "node"),
        ),
        out_specs=(P("feat", "node"), P("feat", "node"), P(None, "feat"), P("feat")),
        check_vma=False,
    )
```

```python
import functools

import jax
import jax.numpy as jnp
from jax import lax
from jax.experimental import pallas as pl
from jax.experimental.pallas import tpu as pltpu
from jax.sharding import PartitionSpec as P

MESH = pl.DeviceIdType.MESH
VMEM = pltpu.VMEM
BF16 = jnp.bfloat16
F32 = jnp.float32
TILE = 128
GROUP = 8
LONG = 32


def around():
    n, f = lax.axis_index("node"), lax.axis_index("feat")
    nx = lax.axis_size("node") // 2
    x, y = lax.rem(n, nx), n // nx

    def at(dx, dy):
        return (lax.rem(y + dy, 2)) * nx + lax.rem(x + dx + nx, nx)

    return n, f, at


def remote(src, dst, send, recv, node, feat):
    return pltpu.make_async_remote_copy(
        src_ref=src, dst_ref=dst, send_sem=send, recv_sem=recv, device_id=(node, feat), device_id_type=MESH
    )


def greet(places):
    barrier = pltpu.get_barrier_semaphore()
    for place in places:
        pl.semaphore_signal(barrier, inc=1, device_id=place, device_id_type=MESH)


def met(places):
    pl.semaphore_wait(pltpu.get_barrier_semaphore(), len(places))


def lanes(t, width):
    return pl.ds(pl.multiple_of(t * width, width), width)


class Sender:
    def __init__(self):
        self.sent = []

    def push(self, src, dst, send, recv, node, feat):
        self.sent.append(remote(src, dst, send, recv, node, feat))
        self.sent[-1].start()

    def arrived(self, dst, send, recv):
        remote(dst, dst, send, recv, lax.axis_index("node"), lax.axis_index("feat")).wait_recv()

    def finish(self):
        for copy in self.sent:
            copy.wait_send()


def ring(f, n_feat):
    if n_feat != 16:
        return [(d, lax.rem(f + d, n_feat), lax.rem(f - d + n_feat, n_feat)) for d in range(1, n_feat)]
    z, y, core = f // 4, lax.rem(f // 2, 2), lax.rem(f, 2)

    def by(dz, dy, dc):
        return lax.rem(z + dz + 4, 4) * 4 + lax.rem(y + dy, 2) * 2 + lax.rem(core + dc, 2)

    offsets = [(dz, dy, dc) for dz in (2, 1, 3, 0) for dy in (1, 0) for dc in (1, 0)][:-1]
    offsets.sort(key=lambda d: -(min(d[0], 4 - d[0]) + 2 * d[1] + d[2]))
    return [(dz * 4 + dy * 2 + dc, by(dz, dy, dc), by(-dz, dy, dc)) for dz, dy, dc in offsets]


def everyone(n, f, at, partners):
    near = [(at(1, 0), f), (at(-1, 0), f), (at(0, 1), f)]
    return near + [(n, p) for _, p, _ in partners]


def split(x):
    high = x.astype(BF16).astype(F32)
    mid = (x - high).astype(BF16).astype(F32)
    lane = lax.broadcasted_iota(jnp.int32, x.shape, 1)
    rest = jnp.where(lane == 1, mid, jnp.where(lane == 2, x - high - mid, 0.0))
    return jnp.where(lane == 0, high, rest).astype(BF16)


def by_tile(x_ref, out_ref):
    for t in range(out_ref.shape[0]):
        out_ref[t] = x_ref[:, t * TILE:(t + 1) * TILE]


def own_products(index, x_ref, tiles, n, out_ref, dims):
    @pl.loop(0, out_ref.shape[0] // GROUP)
    def _(c):
        for u in range(GROUP):
            k = c * GROUP + u
            x = x_ref[index(k)]
            out_ref[k] = lax.dot_general(x, tiles[n * out_ref.shape[0] + k], (dims, ((), ())), preferred_element_type=F32)


def slot_list(count, rows, cols, n, n_node, row_tiles, out_ref):
    slots = rows.shape[2]
    width = out_ref.shape[1]
    q = lax.broadcasted_iota(jnp.int32, (slots, width), 1)
    k = lax.broadcasted_iota(jnp.int32, (slots, width), 0)
    line = lax.broadcasted_iota(jnp.int32, (8, slots), 0)
    number = lax.broadcasted_iota(jnp.int32, (8, slots), 1)
    total = jnp.zeros((8, width), F32)
    base = 0
    for s in range(1, n_node):
        j = lax.rem(n + s, n_node)
        used = count[0, j]
        hit = jnp.where((q == k + base) & (k < used), 1.0, 0.0).astype(BF16)
        mine = jnp.where(line == 0, number, jnp.where(line == 1, j, 0))
        mine = jnp.where(line == 2, rows[0, pl.ds(j, 1)], jnp.where(line == 3, cols[0, pl.ds(j, 1)], mine))
        total = total + jnp.dot(mine.astype(F32).astype(BF16), hit, preferred_element_type=F32)
        base = base + used
    out_ref[...] = jnp.where(
        lax.broadcasted_iota(jnp.int32, out_ref.shape, 0) == 6, base, total.astype(jnp.int32)
    )
    whole = total.astype(jnp.int32)
    out_ref[0:1] = whole[0:1] + whole[1:2] * slots
    out_ref[7:8] = whole[1:2] * row_tiles + whole[3:4]
    out_ref[4:5, :slots] = rows[0, pl.ds(n, 1)]
    out_ref[5:6, :slots] = cols[0, pl.ds(n, 1)]


def gather_kernel(
    x_ref, tiles_ref, cot_ref, count_ref, rows_ref, cols_ref, wt_ref, bias_ref,
    all_ref, tiles, made, cin, win, list_out,
    x_own, x_tiles, count, cols, rows_in, cols_in, wt, bias_in, wst,
    local_sem, tile_sem, send, recv, c_send, c_recv, w_send, w_recv,
):
    n, f, at = around()
    n_feat, channels, span = cin.shape
    inputs = wt_ref.shape[1]
    n_node = count_ref.shape[1]
    slots = made.shape[0]
    half = x_ref.shape[1] // 2
    right, left, other, far = at(1, 0), at(-1, 0), at(0, 1), at(2, 0)
    link = Sender()
    here = [
        pltpu.make_async_copy(src, dst, local_sem.at[i])
        for i, (src, dst) in enumerate([
            (wt_ref, wt), (bias_ref, bias_in), (count_ref, count), (rows_ref, rows_in), (cols_ref, cols_in),
            (cols_ref, cols), (x_ref, x_own),
            (x_ref, all_ref.at[n]), (cot_ref.at[:, lanes(f, span)], cin.at[f]),
        ])
    ]
    moved = [
        pltpu.make_async_copy(
            tiles_ref.at[pl.ds(j * slots, slots)], tiles.at[pl.ds(j * slots, slots)], tile_sem.at[s]
        )
        for s, j in enumerate([n] + [lax.rem(n + s, n_node) for s in range(1, n_node)])
    ]
    partners = ring(f, n_feat)
    places = everyone(n, f, at, partners)
    greet(places)
    for copy in here:
        copy.start()
    met(places)

    low, high = pl.ds(0, half), pl.ds(half, half)

    def push(m, part, k, to, src=None):
        block = all_ref.at[m, :, part]
        link.push(block if src is None else src.at[:, part], block, send.at[k], recv.at[k], to, f)

    def arrived(m, part, k):
        link.arrived(all_ref.at[m, :, part], send.at[k], recv.at[k])

    push(n, low, 0, right, x_ref)
    push(n, high, 1, left, x_ref)
    push(n, low, 2, other, x_ref)
    push(n, high, 3, right, x_ref)
    push(n, low, 4, left, x_ref)
    push(n, high, 5, other, x_ref)
    for d, p, _ in partners:
        link.push(cot_ref.at[:, lanes(p, span)], cin.at[f], c_send.at[d], c_recv.at[d], n, p)
    for copy in here[:2]:
        copy.wait()
    wst[0] = wt[...]
    wst[1] = split(jnp.broadcast_to(bias_in[...], (inputs, channels)).T)
    win[f] = wst[...]
    for d, p, _ in partners:
        link.push(wst, win.at[f], w_send.at[d], w_recv.at[d], n, p)
    for copy in moved:
        copy.start()
    arrived(left, low, 0)
    push(left, low, 6, right)
    arrived(right, high, 1)
    push(right, high, 7, left)
    arrived(other, low, 2)
    push(other, low, 8, right)
    push(other, low, 9, left)
    arrived(other, high, 5)
    push(other, high, 10, right)
    push(other, high, 11, left)
    for copy in here[2:7]:
        copy.wait()
    slot_list(count, rows_in, cols_in, n, n_node, x_tiles.shape[0], list_out)
    arrived(far, low, 6)
    push(far, low, 12, other)
    arrived(far, high, 7)
    push(far, high, 13, other)
    moved[0].wait()
    by_tile(x_own, x_tiles)
    own_products(lambda k: cols[0, n, k], x_tiles, tiles, n, made, ((1,), (1,)))
    arrived(left, high, 3)
    arrived(right, low, 4)
    for m, k in ((at(-1, 1), 0), (at(1, 1), 1)):
        arrived(m, low, 8 + k)
        arrived(m, high, 10 + k)
    for d, _, p in partners:
        link.arrived(cin.at[p], c_send.at[d], c_recv.at[d])
        link.arrived(win.at[p], w_send.at[d], w_recv.at[d])
    for copy in here[7:] + moved[1:]:
        copy.wait()
    arrived(at(2, 1), low, 12)
    arrived(at(2, 1), high, 13)
    link.finish()


def add_products(listed, line, tiles, source, acc, dims):
    total = listed[6, 0]

    @pl.loop(0, (total + (LONG - 1)) // LONG)
    def _(c):
        made = []
        for u in range(LONG):
            q = c * LONG + u
            x = source(q)
            x = jnp.where(q < total, x, jnp.zeros_like(x))
            made.append(
                lax.dot_general(x, tiles[listed[0, q]], (dims, ((), ())), preferred_element_type=F32)
            )
        for u in range(LONG):
            t = listed[line, c * LONG + u]
            acc[t] = acc[t] + made[u]


def place_products(listed, line, made, acc):
    @pl.loop(0, made.shape[0] // GROUP)
    def _(c):
        for u in range(GROUP):
            t = listed[line, c * GROUP + u]
            acc[t] = acc[t] + made[c * GROUP + u]


def forward_kernel(list_ref, x_ref, tiles, made, z_ref, acc, listed, sem):
    moved = pltpu.make_async_copy(list_ref, listed, sem)
    moved.start()
    n = lax.axis_index("node")
    for t in range(acc.shape[0]):
        acc[t] = x_ref[n, :, t * TILE:(t + 1) * TILE].astype(F32)
    moved.wait()
    place_products(listed, 4, made, acc)
    add_products(
        listed, 2, tiles, lambda q: x_ref[listed[1, q], :, lanes(listed[3, q], TILE)], acc, ((1,), (1,))
    )
    for t in range(acc.shape[0]):
        z_ref[:, t * TILE:(t + 1) * TILE] = acc[t].astype(BF16)


def dense_kernel(
    norm, z_ref, cin, win,
    h_ref, ost, gst,
    zin, hst,
    z_send, z_recv, h_send, h_recv, own_sem,
):
    n, f, _ = around()
    n_feat, rows, span = zin.shape
    channels, inputs = win.shape[2:]
    hidden = n_feat * channels
    link = Sender()
    partners = ring(f, n_feat)
    places = [(n, p) for _, p, _ in partners]
    greet(places)
    zin[f] = z_ref[:, lanes(f, span)]
    met(places)
    for d, p, _ in partners:
        link.push(z_ref.at[:, lanes(p, span)], zin.at[f], z_send.at[d], z_recv.at[d], n, p)
    wt = win[:, 0].reshape(hidden, inputs)
    bias = jnp.sum(win[:, 1].reshape(hidden, inputs).astype(F32), axis=1, keepdims=True)
    cot = cin[...].reshape(hidden, span)
    w = wt.astype(F32).T.astype(BF16)
    for d, _, p in partners:
        link.arrived(zin.at[p], z_send.at[d], z_recv.at[d])
    z = zin[...].astype(F32).reshape(n_feat * rows, span).astype(BF16)
    parts = []
    for t in range(span // TILE):
        part = slice(t * TILE, (t + 1) * TILE)
        pre = jnp.dot(wt, z[:, part], preferred_element_type=F32) + bias
        s = jax.nn.sigmoid(pre)
        g = (cot[:, part].astype(F32) * s * (1.0 + pre * (1.0 - s))).astype(BF16)
        h = jnp.dot(w, g, preferred_element_type=F32)
        hst[:, :, part] = h.reshape(n_feat, rows, TILE).astype(BF16)
        ost[:, :, part] = (pre * s).astype(BF16).reshape(n_feat, channels, TILE)
        parts.append(g)
    for d, p, _ in partners:
        link.push(hst.at[p], h_ref.at[:, lanes(f, span)], h_send.at[d], h_recv.at[d], n, p)
    own_h = pltpu.make_async_copy(hst.at[f], h_ref.at[:, lanes(f, span)], own_sem)
    own_h.start()
    g = jnp.concatenate(parts, axis=1)
    both = jnp.concatenate([z, jnp.ones_like(z)], axis=0)
    sums = lax.dot_general(g, both, (((1,), (1,)), ((), ())), preferred_element_type=F32) * norm
    gst[:, 0] = sums[:, :inputs].astype(BF16).reshape(n_feat, channels, inputs)
    gst[:, 1] = split(sums[:, inputs:]).reshape(n_feat, channels, inputs)
    for d, _, p in partners:
        link.arrived(h_ref.at[:, lanes(p, span)], h_send.at[d], h_recv.at[d])
    own_h.wait()
    link.finish()


def backward_kernel(list_ref, h_ref, tiles, part_ref, acc, listed, sem):
    moved = pltpu.make_async_copy(list_ref, listed, sem)
    moved.start()
    n_node = part_ref.shape[0]
    row_tiles = acc.shape[0] // n_node
    acc[...] = jnp.zeros_like(acc)
    moved.wait()
    add_products(
        listed, 7, tiles, lambda q: h_ref[:, lanes(listed[2, q], TILE)], acc, ((1,), (0,))
    )
    for j in range(n_node):
        for t in range(row_tiles):
            part_ref[j, :, t * TILE:(t + 1) * TILE] = acc[j * row_tiles + t].astype(BF16)


def reduce_kernel(
    listed, part_ref, h_ref, tiles, gst, ost,
    fl_in, fr_in, fy_in, made, gw_out, gb_out, out_ref,
    far_in, dl_in, dr_in, hl_in, hr_in, hl_out, hr_out, y_out, r_out, l_out, gin, sums, h_tiles,
    send, recv, s_send, s_recv, g_send, g_recv, o_send, o_recv, own_sem,
):
    n, f, at = around()
    n_feat, _, span = ost.shape
    n_node, _, nodes = part_ref.shape
    half = nodes // 2
    right, left, other, far = at(1, 0), at(-1, 0), at(0, 1), at(2, 0)
    link = Sender()
    partners = ring(f, n_feat)
    places = [(lax.rem(n + d, n_node), f) for d in range(1, n_node)] + [(n, p) for _, p, _ in partners]
    greet(places)
    met(places)

    def push(src, dst, k, to):
        link.push(src, dst, send.at[k], recv.at[k], to, f)

    def arrived(dst, k):
        link.arrived(dst, send.at[k], recv.at[k])

    def add(*terms):
        total = terms[0].astype(F32)
        for term in terms[1:]:
            total = total + term.astype(F32)
        return total.astype(BF16)

    low, high = pl.ds(0, half), pl.ds(half, half)
    halves = (low, high)
    for i, part in enumerate(halves):
        push(part_ref.at[at(2, 1), :, part], far_in.at[:, part], i, other)
        push(part_ref.at[at(1, 1), :, part], dl_in.at[:, part], 2 + i, right)
        push(part_ref.at[at(-1, 1), :, part], dr_in.at[:, part], 4 + i, left)
    for d, p, _ in partners:
        link.push(gst.at[p], gin.at[f], g_send.at[d], g_recv.at[d], n, p)
    gin[f] = gst[f]
    own_out = pltpu.make_async_copy(ost.at[f], out_ref.at[:, lanes(f, span)], own_sem)
    own_out.start()
    for d, p, _ in partners:
        link.push(ost.at[p], out_ref.at[:, lanes(f, span)], o_send.at[d], o_recv.at[d], n, p)
    arrived(far_in.at[:, low], 0)
    hl_out[...] = add(part_ref[far, :, low], far_in[:, low])
    push(hl_out, hl_in, 6, right)
    arrived(far_in.at[:, high], 1)
    hr_out[...] = add(part_ref[far, :, high], far_in[:, high])
    push(hr_out, hr_in, 7, left)
    push(part_ref.at[right, :, high], fl_in.at[:, high], 8, right)
    push(part_ref.at[left, :, low], fr_in.at[:, low], 9, left)
    for i, part in enumerate(halves):
        arrived(dl_in.at[:, part], 2 + i)
        arrived(dr_in.at[:, part], 4 + i)
        y_out[:, part] = add(part_ref[other, :, part], dl_in[:, part], dr_in[:, part])
        push(y_out.at[:, part], fy_in.at[:, part], 10 + i, other)
    arrived(hl_in, 6)
    r_out[...] = add(part_ref[right, :, low], hl_in[...])
    push(r_out, fl_in.at[:, low], 12, right)
    arrived(hr_in, 7)
    l_out[...] = add(part_ref[left, :, high], hr_in[...])
    push(l_out, fr_in.at[:, high], 13, left)
    for d, _, p in partners:
        link.arrived(gin.at[p], g_send.at[d], g_recv.at[d])
    sums[n] = jnp.sum(gin[...].astype(F32), axis=0)
    for d in range(1, n_node):
        link.push(sums.at[n], sums.at[n], s_send.at[d], s_recv.at[d], lax.rem(n + d, n_node), f)
    by_tile(h_ref, h_tiles)
    own_products(lambda k: listed[4, k], h_tiles, tiles, n, made, ((1,), (0,)))
    for d in range(1, n_node):
        link.arrived(sums.at[lax.rem(n - d + n_node, n_node)], s_send.at[d], s_recv.at[d])
    total = jnp.sum(sums[...], axis=0)
    gw_out[...] = total[0]
    gb_out[...] = jnp.sum(total[1].T, axis=0, keepdims=True)
    for i, part in enumerate(halves):
        arrived(fy_in.at[:, part], 10 + i)
    arrived(fl_in.at[:, high], 8)
    arrived(fr_in.at[:, low], 9)
    arrived(fl_in.at[:, low], 12)
    arrived(fr_in.at[:, high], 13)
    for d, _, p in partners:
        link.arrived(out_ref.at[:, lanes(p, span)], o_send.at[d], o_recv.at[d])
    own_out.wait()
    link.finish()


def final_kernel(
    list_ref, h_ref, fl, fr, fy, made, gw_ref, gb_ref, made_out,
    gf_ref, gw_out, gb_out, out_ref, acc, listed, sem, out_sem,
):
    scalars = pltpu.make_async_copy(list_ref, listed, sem)
    scalars.start()
    moved = pltpu.make_async_copy(made_out, out_ref, out_sem)
    moved.start()
    for t in range(acc.shape[0]):
        span = slice(t * TILE, (t + 1) * TILE)
        acc[t] = (
            h_ref[:, span].astype(F32) + fl[:, span].astype(F32)
            + fr[:, span].astype(F32) + fy[:, span].astype(F32)
        )
    scalars.wait()
    place_products(listed, 5, made, acc)
    for t in range(acc.shape[0]):
        gf_ref[:, t * TILE:(t + 1) * TILE] = acc[t].astype(BF16)
    gw_out[...] = gw_ref[...]
    gb_out[...] = gb_ref[...]
    moved.wait()


def local(features, weight, bias, tile_values, tile_rows, tile_cols, tile_count, cotangent):
    n_node, n_feat = lax.axis_size("node"), lax.axis_size("feat")
    rows, nodes = features.shape
    inputs, channels = weight.shape
    row_tiles = nodes // TILE
    span = row_tiles // n_feat * TILE
    slots = tile_rows.shape[2]
    dma = pltpu.SemaphoreType.DMA
    in_vmem = pl.BlockSpec(memory_space=VMEM)
    in_smem = pl.BlockSpec(memory_space=pltpu.SMEM)
    in_hbm = pl.BlockSpec(memory_space=pltpu.HBM)
    shape = jax.ShapeDtypeStruct
    block = (rows, nodes)
    pair = (2, channels, inputs)

    def params(mib, **more):
        return pltpu.CompilerParams(vmem_limit_bytes=mib << 20, **more)

    def keep(x):
        return pltpu.with_memory_space_constraint(x, pltpu.HBM)

    def pairs(k):
        return [dma((n_feat,))] * k

    x_all, tiles, made, cin, win, listed = pl.pallas_call(
        gather_kernel,
        out_shape=(
            shape((n_node,) + block, BF16),
            shape((n_node * slots, TILE, TILE), BF16),
            shape((slots, rows, TILE), F32),
            shape((n_feat, channels, span), BF16),
            shape((n_feat,) + pair, BF16),
            shape((8, n_node * slots), jnp.int32),
        ),
        in_specs=[in_hbm] * 8,
        out_specs=(in_vmem,) * 6,
        scratch_shapes=[
            VMEM(block, BF16), VMEM((row_tiles, rows, TILE), BF16),
            pltpu.SMEM(tile_count.shape, jnp.int32), pltpu.SMEM(tile_cols.shape, jnp.int32),
            VMEM(tile_rows.shape, jnp.int32), VMEM(tile_cols.shape, jnp.int32),
            VMEM((channels, inputs), BF16), VMEM((1, channels), F32), VMEM(pair, BF16),
            dma((9,)), dma((n_node,)), dma((14,)), dma((14,)),
        ] + pairs(4),
        compiler_params=params(20, collective_id=0, has_side_effects=True),
        name="gather",
    )(
        keep(features), keep(tile_values.reshape(n_node * slots, TILE, TILE)), keep(cotangent),
        keep(tile_count), keep(tile_rows), keep(tile_cols),
        keep(weight.T), keep(bias.reshape(1, channels)),
    )

    acc = VMEM((row_tiles, rows, TILE), F32)
    scalars = [pltpu.SMEM((8, n_node * slots), jnp.int32), dma(())]
    z = pl.pallas_call(
        forward_kernel,
        out_shape=shape(block, BF16),
        in_specs=[in_vmem] * 4,
        out_specs=in_vmem,
        scratch_shapes=[acc] + scalars,
        compiler_params=params(16),
        name="forward",
    )(listed, x_all, tiles, made)

    h, ost, gst = pl.pallas_call(
        functools.partial(dense_kernel, 1.0 / float(nodes * n_node) ** 0.5),
        out_shape=(
            shape(block, BF16),
            shape((n_feat, channels, span), BF16),
            shape((n_feat,) + pair, BF16),
        ),
        in_specs=[in_vmem] * 3,
        out_specs=(in_vmem,) * 3,
        scratch_shapes=[
            VMEM((n_feat, rows, span), BF16),
            VMEM((n_feat, rows, span), BF16),
        ] + pairs(4) + [dma(())],
        compiler_params=params(16, collective_id=1, has_side_effects=True),
        name="dense",
    )(z, cin, win)

    part = pl.pallas_call(
        backward_kernel,
        out_shape=shape((n_node,) + block, BF16),
        in_specs=[in_vmem] * 3,
        out_specs=in_vmem,
        scratch_shapes=[VMEM((n_node * row_tiles, rows, TILE), F32)] + scalars,
        compiler_params=params(16),
        name="backward",
    )(listed, h, tiles)

    whole, half = VMEM(block, BF16), VMEM((rows, nodes // 2), BF16)
    fl, fr, fy, made, gwt, gb, out = pl.pallas_call(
        reduce_kernel,
        out_shape=(
            shape(block, BF16),
            shape(block, BF16),
            shape(block, BF16),
            shape((slots, rows, TILE), F32),
            shape((channels, inputs), F32),
            shape((1, channels), F32),
            shape((channels, nodes), BF16),
        ),
        in_specs=[in_smem] + [in_vmem] * 5,
        out_specs=(in_vmem,) * 7,
        scratch_shapes=[whole] * 3 + [half] * 4 + [whole] + [half] * 2 + [
            VMEM((n_feat,) + pair, BF16), VMEM((n_node,) + pair, F32),
            VMEM((row_tiles, rows, TILE), BF16),
            dma((14,)), dma((14,)), dma((n_node,)), dma((n_node,)),
        ] + pairs(4) + [dma(())],
        compiler_params=params(16, collective_id=2, has_side_effects=True),
        name="reduce",
    )(listed, part, h, tiles, gst, ost)

    gf, gwt, gb, out = pl.pallas_call(
        final_kernel,
        out_shape=(
            shape(block, BF16),
            shape((channels, inputs), F32),
            shape((1, channels), F32),
            shape((channels, nodes), BF16),
        ),
        in_specs=[in_vmem] * 9,
        out_specs=(in_vmem,) * 3 + (in_hbm,),
        scratch_shapes=[acc] + scalars + [dma(())],
        compiler_params=params(16),
        name="final",
    )(listed, h, fl, fr, fy, made, gwt, gb, out)
    return out, gf, gwt.T, gb.reshape(channels)


def solution(mesh):
    return jax.shard_map(
        local,
        mesh=mesh,
        in_specs=(
            P("feat", "node"),
            P(None, "feat"),
            P("feat"),
            P("node", None, None, None, None),
            P("node", None, None),
            P("node", None, None),
            P("node", None),
            P("feat", "node"),
        ),
        out_specs=(P("feat", "node"), P("feat", "node"), P(None, "feat"), P("feat")),
        check_vma=False,
    )
```

```python
import functools

import jax
import jax.numpy as jnp
from jax import lax
from jax.experimental import pallas as pl
from jax.experimental.pallas import tpu as pltpu
from jax.sharding import PartitionSpec as P

MESH = pl.DeviceIdType.MESH
VMEM = pltpu.VMEM
BF16 = jnp.bfloat16
F32 = jnp.float32
TILE = 128
GROUP = 48
LONG = 32


def around():
    n, f = lax.axis_index("node"), lax.axis_index("feat")
    nx = lax.axis_size("node") // 2
    x, y = lax.rem(n, nx), n // nx

    def at(dx, dy):
        return (lax.rem(y + dy, 2)) * nx + lax.rem(x + dx + nx, nx)

    return n, f, at


def remote(src, dst, send, recv, node, feat):
    return pltpu.make_async_remote_copy(
        src_ref=src, dst_ref=dst, send_sem=send, recv_sem=recv, device_id=(node, feat), device_id_type=MESH
    )


def greet(places):
    barrier = pltpu.get_barrier_semaphore()
    for place in places:
        pl.semaphore_signal(barrier, inc=1, device_id=place, device_id_type=MESH)


def met(places):
    pl.semaphore_wait(pltpu.get_barrier_semaphore(), len(places))


def lanes(t, width):
    return pl.ds(pl.multiple_of(t * width, width), width)


class Sender:
    def __init__(self):
        self.sent = []

    def push(self, src, dst, send, recv, node, feat):
        self.sent.append(remote(src, dst, send, recv, node, feat))
        self.sent[-1].start()

    def arrived(self, dst, send, recv):
        remote(dst, dst, send, recv, lax.axis_index("node"), lax.axis_index("feat")).wait_recv()

    def finish(self):
        for copy in self.sent:
            copy.wait_send()


def ring(f, n_feat):
    if n_feat != 16:
        return [(d, lax.rem(f + d, n_feat), lax.rem(f - d + n_feat, n_feat)) for d in range(1, n_feat)]
    z, y, core = f // 4, lax.rem(f // 2, 2), lax.rem(f, 2)

    def by(dz, dy, dc):
        return lax.rem(z + dz + 4, 4) * 4 + lax.rem(y + dy, 2) * 2 + lax.rem(core + dc, 2)

    offsets = [(dz, dy, dc) for dz in (2, 1, 3, 0) for dy in (1, 0) for dc in (1, 0)][:-1]
    offsets.sort(key=lambda d: -(min(d[0], 4 - d[0]) + 2 * d[1] + d[2]))
    return [(dz * 4 + dy * 2 + dc, by(dz, dy, dc), by(-dz, dy, dc)) for dz, dy, dc in offsets]


def everyone(n, f, at, partners):
    near = [(at(1, 0), f), (at(-1, 0), f), (at(0, 1), f)]
    return near + [(n, p) for _, p, _ in partners]


def split(x):
    high = x.astype(BF16).astype(F32)
    mid = (x - high).astype(BF16).astype(F32)
    lane = lax.broadcasted_iota(jnp.int32, x.shape, 1)
    rest = jnp.where(lane == 1, mid, jnp.where(lane == 2, x - high - mid, 0.0))
    return jnp.where(lane == 0, high, rest).astype(BF16)


def by_tile(x_ref, upper, lower):
    rows = x_ref.shape[0]
    none = jnp.zeros((rows, TILE), F32)
    for t in range(upper.shape[0]):
        x = x_ref[:, t * TILE:(t + 1) * TILE].astype(F32)
        upper[t] = jnp.concatenate([x, none], axis=0).astype(BF16)
        lower[t] = jnp.concatenate([none, x], axis=0).astype(BF16)


def two(x, y, a, b, across):
    pair = jnp.concatenate([x, y], axis=1)
    both = jnp.concatenate([a, b], axis=across)
    return lax.dot_general(pair, both, (((1,), (across,)), ((), ())), preferred_element_type=F32)


def own_products(index, upper, lower, tiles, first, out_ref):
    rows = out_ref.shape[1]

    @pl.loop(0, out_ref.shape[0] // GROUP)
    def _(c):
        for u in range(0, GROUP, 2):
            k = c * GROUP + u
            made = two(upper[index(k)], lower[index(k + 1)], tiles[first + k], tiles[first + k + 1], 0)
            out_ref[k] = made[:rows]
            out_ref[k + 1] = made[rows:]


def slot_list(count, rows, cols, n, n_node, row_tiles, out_ref):
    slots = rows.shape[2]
    width = out_ref.shape[1]
    q = lax.broadcasted_iota(jnp.int32, (slots, width), 1)
    k = lax.broadcasted_iota(jnp.int32, (slots, width), 0)
    line = lax.broadcasted_iota(jnp.int32, (8, slots), 0)
    number = lax.broadcasted_iota(jnp.int32, (8, slots), 1)
    total = jnp.zeros((8, width), F32)
    base = 0
    for s in range(1, n_node):
        j = lax.rem(n + s, n_node)
        used = count[0, j]
        hit = jnp.where((q == k + base) & (k < used), 1.0, 0.0).astype(BF16)
        mine = jnp.where(line == 0, number, jnp.where(line == 1, j, 0))
        mine = jnp.where(line == 2, rows[0, pl.ds(j, 1)], jnp.where(line == 3, cols[0, pl.ds(j, 1)], mine))
        total = total + jnp.dot(mine.astype(F32).astype(BF16), hit, preferred_element_type=F32)
        base = base + used
    out_ref[...] = jnp.where(
        lax.broadcasted_iota(jnp.int32, out_ref.shape, 0) == 6, base, total.astype(jnp.int32)
    )
    whole = total.astype(jnp.int32)
    out_ref[0:1] = whole[0:1] + whole[1:2] * slots
    out_ref[7:8] = whole[1:2] * row_tiles + whole[3:4]
    out_ref[4:5, :slots] = rows[0, pl.ds(n, 1)]
    out_ref[5:6, :slots] = cols[0, pl.ds(n, 1)]


def products(x_ref, upper, lower, cols, j, tiles, out_ref):
    by_tile(x_ref, upper, lower)
    rows = x_ref.shape[0]
    slots = out_ref.shape[0] // rows

    @pl.loop(0, slots // GROUP)
    def _(c):
        for u in range(0, GROUP, 2):
            k = c * GROUP + u
            out_ref[pl.ds(pl.multiple_of(k * rows, rows), 2 * rows)] = two(
                upper[cols[0, j, k]], lower[cols[0, j, k + 1]],
                tiles[j * slots + k], tiles[j * slots + k + 1], 1,
            )


def sum_rows(count, rows_in, j, made, z_ref):
    slots = rows_in.shape[2]
    rows = made.shape[0] // slots
    row_tiles = z_ref.shape[0] // rows
    t = lax.broadcasted_iota(jnp.int32, (row_tiles, slots), 0)
    k = lax.broadcasted_iota(jnp.int32, (row_tiles, slots), 1)
    hit = jnp.where((t == rows_in[0, pl.ds(j, 1)]) & (k < count[0, j]), 1.0, 0.0).astype(BF16)
    for c in range(rows):
        part = made[pl.ds(c, slots, stride=rows), :]
        high = part.astype(BF16)
        low = (part - high.astype(F32)).astype(BF16)
        where = pl.ds(c, row_tiles, stride=rows)
        z_ref[where, :] = z_ref[where, :] + (
            jnp.dot(hit, high, preferred_element_type=F32) + jnp.dot(hit, low, preferred_element_type=F32)
        )


def forward_kernel(
    norm, x_ref, tiles_ref, cot_ref, count_ref, rows_ref, cols_ref, wt_ref, bias_ref,
    tiles, list_out, h_ref, ost, gst,
    x_all, x_own, upper, lower, made, z_sum, z_ref, zin, hst, cin, win,
    count, cols, rows_in, cols_in, wt_in, bias_in, wst,
    local_sem, tile_sem, own_sem, send, recv, c_send, c_recv, w_send, w_recv, z_send, z_recv, h_send, h_recv,
):
    n, f, at = around()
    n_feat, channels, span = cin.shape
    rows = x_ref.shape[0]
    inputs = wt_ref.shape[1]
    hidden = n_feat * channels
    n_node = count_ref.shape[1]
    slots = tiles.shape[0] // n_node
    half = x_ref.shape[1] // 2
    right, left, other, far = at(1, 0), at(-1, 0), at(0, 1), at(2, 0)
    order = [n, left, right, other, far, at(-1, 1), at(1, 1), at(2, 1)]
    link = Sender()
    here = [
        pltpu.make_async_copy(src, dst, local_sem.at[i])
        for i, (src, dst) in enumerate([
            (wt_ref, wt_in), (bias_ref, bias_in), (count_ref, count), (rows_ref, rows_in), (cols_ref, cols_in),
            (cols_ref, cols), (x_ref, x_own), (cot_ref.at[:, lanes(f, span)], cin.at[f]),
        ])
    ]
    moved = [
        pltpu.make_async_copy(
            tiles_ref.at[pl.ds(j * slots, slots)], tiles.at[pl.ds(j * slots, slots)], tile_sem.at[s]
        )
        for s, j in enumerate(order)
    ]
    partners = ring(f, n_feat)
    places = everyone(n, f, at, partners)
    greet(places)
    for copy in here:
        copy.start()
    met(places)

    low, high = pl.ds(0, half), pl.ds(half, half)

    def push(m, part, k, to, src=None):
        block = x_all.at[m, :, part]
        link.push(block if src is None else src.at[:, part], block, send.at[k], recv.at[k], to, f)

    def arrived(m, part, k):
        link.arrived(x_all.at[m, :, part], send.at[k], recv.at[k])

    def work(s):
        moved[s].wait()
        products(x_own if s == 0 else x_all.at[order[s]], upper, lower, cols, order[s], tiles, made)
        sum_rows(count, rows_in, order[s], made, z_sum)

    push(n, low, 0, right, x_ref)
    push(n, high, 1, left, x_ref)
    push(n, low, 2, other, x_ref)
    push(n, high, 3, right, x_ref)
    push(n, low, 4, left, x_ref)
    push(n, high, 5, other, x_ref)
    for d, p, _ in partners:
        link.push(cot_ref.at[:, lanes(p, span)], cin.at[f], c_send.at[d], c_recv.at[d], n, p)
    for copy in here[:2]:
        copy.wait()
    wst[0] = wt_in[...]
    wst[1] = split(jnp.broadcast_to(bias_in[...], (inputs, channels)).T)
    win[f] = wst[...]
    for d, p, _ in partners:
        link.push(wst, win.at[f], w_send.at[d], w_recv.at[d], n, p)
    for copy in moved:
        copy.start()
    for copy in here[2:]:
        copy.wait()
    for t in range(upper.shape[0]):
        z_sum[t * rows:(t + 1) * rows] = x_own[:, t * TILE:(t + 1) * TILE].astype(F32)
    work(0)
    arrived(left, low, 0)
    push(left, low, 6, right)
    arrived(right, high, 1)
    push(right, high, 7, left)
    arrived(other, low, 2)
    push(other, low, 8, right)
    push(other, low, 9, left)
    arrived(other, high, 5)
    push(other, high, 10, right)
    push(other, high, 11, left)
    arrived(left, high, 3)
    work(1)
    arrived(far, low, 6)
    push(far, low, 12, other)
    arrived(far, high, 7)
    push(far, high, 13, other)
    arrived(right, low, 4)
    work(2)
    work(3)
    work(4)
    arrived(at(-1, 1), low, 8)
    arrived(at(-1, 1), high, 10)
    work(5)
    arrived(at(1, 1), low, 9)
    arrived(at(1, 1), high, 11)
    work(6)
    arrived(at(2, 1), low, 12)
    arrived(at(2, 1), high, 13)
    work(7)
    for t in range(upper.shape[0]):
        z_ref[:, t * TILE:(t + 1) * TILE] = z_sum[t * rows:(t + 1) * rows].astype(BF16)
    for d, p, _ in partners:
        link.push(z_ref.at[:, lanes(p, span)], zin.at[f], z_send.at[d], z_recv.at[d], n, p)
    zin[f] = z_ref[:, lanes(f, span)]
    slot_list(count, rows_in, cols_in, n, n_node, upper.shape[0], list_out)
    for d, _, p in partners:
        link.arrived(cin.at[p], c_send.at[d], c_recv.at[d])
        link.arrived(win.at[p], w_send.at[d], w_recv.at[d])
    wt = win[:, 0].reshape(hidden, inputs)
    bias = jnp.sum(win[:, 1].reshape(hidden, inputs).astype(F32), axis=1, keepdims=True)
    cot = cin[...].reshape(hidden, span)
    w = wt.astype(F32).T.astype(BF16)
    for d, _, p in partners:
        link.arrived(zin.at[p], z_send.at[d], z_recv.at[d])
    z = zin[...].astype(F32).reshape(n_feat * rows, span).astype(BF16)
    parts = []
    for t in range(span // TILE):
        part = slice(t * TILE, (t + 1) * TILE)
        pre = jnp.dot(wt, z[:, part], preferred_element_type=F32) + bias
        s = jax.nn.sigmoid(pre)
        g = (cot[:, part].astype(F32) * s * (1.0 + pre * (1.0 - s))).astype(BF16)
        h = jnp.dot(w, g, preferred_element_type=F32)
        hst[:, :, part] = h.reshape(n_feat, rows, TILE).astype(BF16)
        ost[:, :, part] = (pre * s).astype(BF16).reshape(n_feat, channels, TILE)
        parts.append(g)
    for d, p, _ in partners:
        link.push(hst.at[p], h_ref.at[:, lanes(f, span)], h_send.at[d], h_recv.at[d], n, p)
    own_h = pltpu.make_async_copy(hst.at[f], h_ref.at[:, lanes(f, span)], own_sem)
    own_h.start()
    g = jnp.concatenate(parts, axis=1)
    both = jnp.concatenate([z, jnp.ones_like(z)], axis=0)
    sums = lax.dot_general(g, both, (((1,), (1,)), ((), ())), preferred_element_type=F32) * norm
    gst[:, 0] = sums[:, :inputs].astype(BF16).reshape(n_feat, channels, inputs)
    gst[:, 1] = split(sums[:, inputs:]).reshape(n_feat, channels, inputs)
    for d, _, p in partners:
        link.arrived(h_ref.at[:, lanes(p, span)], h_send.at[d], h_recv.at[d])
    own_h.wait()
    link.finish()


def add_products(listed, source, target, upper, lower, tiles, acc):
    total = listed[6, 0]
    rows = acc.shape[1]

    def used(x, q):
        return jnp.where(q < total, x, jnp.zeros_like(x))

    @pl.loop(0, (total + (LONG - 1)) // LONG)
    def _(c):
        made = []
        for u in range(0, LONG, 2):
            q = c * LONG + u
            made.append(two(
                used(upper[listed[source, q]], q), used(lower[listed[source, q + 1]], q + 1),
                tiles[listed[0, q]], tiles[listed[0, q + 1]], 0,
            ))
        for u in range(LONG):
            t = listed[target, c * LONG + u]
            part = made[u // 2]
            acc[t] = acc[t] + (part[:rows] if u % 2 == 0 else part[rows:])


def place_products(listed, line, made, acc):
    @pl.loop(0, made.shape[0] // GROUP)
    def _(c):
        for u in range(GROUP):
            t = listed[line, c * GROUP + u]
            acc[t] = acc[t] + made[c * GROUP + u]


def backward_kernel(list_ref, h_ref, tiles, part_ref, acc, upper, lower, listed, sem):
    moved = pltpu.make_async_copy(list_ref, listed, sem)
    moved.start()
    n_node = part_ref.shape[0]
    row_tiles = acc.shape[0] // n_node
    acc[...] = jnp.zeros_like(acc)
    by_tile(h_ref, upper, lower)
    moved.wait()
    add_products(listed, 2, 7, upper, lower, tiles, acc)
    for j in range(n_node):
        for t in range(row_tiles):
            part_ref[j, :, t * TILE:(t + 1) * TILE] = acc[j * row_tiles + t].astype(BF16)


def reduce_kernel(
    listed, part_ref, h_ref, tiles, gst, ost,
    fl_in, fr_in, fy_in, made, gw_out, gb_out, out_ref,
    far_in, dl_in, dr_in, hl_in, hr_in, hl_out, hr_out, y_out, r_out, l_out, gin, sums, upper, lower,
    send, recv, s_send, s_recv, g_send, g_recv, o_send, o_recv, own_sem,
):
    n, f, at = around()
    n_feat, _, span = ost.shape
    n_node, _, nodes = part_ref.shape
    half = nodes // 2
    right, left, other, far = at(1, 0), at(-1, 0), at(0, 1), at(2, 0)
    link = Sender()
    partners = ring(f, n_feat)
    places = [(lax.rem(n + d, n_node), f) for d in range(1, n_node)] + [(n, p) for _, p, _ in partners]
    greet(places)
    met(places)

    def push(src, dst, k, to):
        link.push(src, dst, send.at[k], recv.at[k], to, f)

    def arrived(dst, k):
        link.arrived(dst, send.at[k], recv.at[k])

    def add(*terms):
        total = terms[0].astype(F32)
        for term in terms[1:]:
            total = total + term.astype(F32)
        return total.astype(BF16)

    low, high = pl.ds(0, half), pl.ds(half, half)
    halves = (low, high)
    for i, part in enumerate(halves):
        push(part_ref.at[at(2, 1), :, part], far_in.at[:, part], i, other)
        push(part_ref.at[at(1, 1), :, part], dl_in.at[:, part], 2 + i, right)
        push(part_ref.at[at(-1, 1), :, part], dr_in.at[:, part], 4 + i, left)
    for d, p, _ in partners:
        link.push(gst.at[p], gin.at[f], g_send.at[d], g_recv.at[d], n, p)
    gin[f] = gst[f]
    own_out = pltpu.make_async_copy(ost.at[f], out_ref.at[:, lanes(f, span)], own_sem)
    own_out.start()
    for d, p, _ in partners:
        link.push(ost.at[p], out_ref.at[:, lanes(f, span)], o_send.at[d], o_recv.at[d], n, p)
    arrived(far_in.at[:, low], 0)
    hl_out[...] = add(part_ref[far, :, low], far_in[:, low])
    push(hl_out, hl_in, 6, right)
    arrived(far_in.at[:, high], 1)
    hr_out[...] = add(part_ref[far, :, high], far_in[:, high])
    push(hr_out, hr_in, 7, left)
    push(part_ref.at[right, :, high], fl_in.at[:, high], 8, right)
    push(part_ref.at[left, :, low], fr_in.at[:, low], 9, left)
    for i, part in enumerate(halves):
        arrived(dl_in.at[:, part], 2 + i)
        arrived(dr_in.at[:, part], 4 + i)
        y_out[:, part] = add(part_ref[other, :, part], dl_in[:, part], dr_in[:, part])
        push(y_out.at[:, part], fy_in.at[:, part], 10 + i, other)
    arrived(hl_in, 6)
    r_out[...] = add(part_ref[right, :, low], hl_in[...])
    push(r_out, fl_in.at[:, low], 12, right)
    arrived(hr_in, 7)
    l_out[...] = add(part_ref[left, :, high], hr_in[...])
    push(l_out, fr_in.at[:, high], 13, left)
    for d, _, p in partners:
        link.arrived(gin.at[p], g_send.at[d], g_recv.at[d])
    sums[n] = jnp.sum(gin[...].astype(F32), axis=0)
    for d in range(1, n_node):
        link.push(sums.at[n], sums.at[n], s_send.at[d], s_recv.at[d], lax.rem(n + d, n_node), f)
    by_tile(h_ref, upper, lower)
    own_products(lambda k: listed[4, k], upper, lower, tiles, n * made.shape[0], made)
    for d in range(1, n_node):
        link.arrived(sums.at[lax.rem(n - d + n_node, n_node)], s_send.at[d], s_recv.at[d])
    total = jnp.sum(sums[...], axis=0)
    gw_out[...] = total[0]
    gb_out[...] = jnp.sum(total[1].T, axis=0, keepdims=True)
    for i, part in enumerate(halves):
        arrived(fy_in.at[:, part], 10 + i)
    arrived(fl_in.at[:, high], 8)
    arrived(fr_in.at[:, low], 9)
    arrived(fl_in.at[:, low], 12)
    arrived(fr_in.at[:, high], 13)
    for d, _, p in partners:
        link.arrived(out_ref.at[:, lanes(p, span)], o_send.at[d], o_recv.at[d])
    own_out.wait()
    link.finish()


def final_kernel(
    list_ref, h_ref, fl, fr, fy, made, gw_ref, gb_ref, made_out,
    gf_ref, gw_out, gb_out, out_ref, acc, listed, sem, out_sem,
):
    scalars = pltpu.make_async_copy(list_ref, listed, sem)
    scalars.start()
    moved = pltpu.make_async_copy(made_out, out_ref, out_sem)
    moved.start()
    for t in range(acc.shape[0]):
        span = slice(t * TILE, (t + 1) * TILE)
        acc[t] = (
            h_ref[:, span].astype(F32) + fl[:, span].astype(F32)
            + fr[:, span].astype(F32) + fy[:, span].astype(F32)
        )
    scalars.wait()
    place_products(listed, 5, made, acc)
    for t in range(acc.shape[0]):
        gf_ref[:, t * TILE:(t + 1) * TILE] = acc[t].astype(BF16)
    gw_out[...] = gw_ref[...]
    gb_out[...] = gb_ref[...]
    moved.wait()


def local(features, weight, bias, tile_values, tile_rows, tile_cols, tile_count, cotangent):
    n_node, n_feat = lax.axis_size("node"), lax.axis_size("feat")
    rows, nodes = features.shape
    inputs, channels = weight.shape
    row_tiles = nodes // TILE
    span = row_tiles // n_feat * TILE
    slots = tile_rows.shape[2]
    dma = pltpu.SemaphoreType.DMA
    in_vmem = pl.BlockSpec(memory_space=VMEM)
    in_smem = pl.BlockSpec(memory_space=pltpu.SMEM)
    in_hbm = pl.BlockSpec(memory_space=pltpu.HBM)
    shape = jax.ShapeDtypeStruct
    block = (rows, nodes)
    pair = (2, channels, inputs)

    def params(mib, **more):
        return pltpu.CompilerParams(vmem_limit_bytes=mib << 20, **more)

    def keep(x):
        return pltpu.with_memory_space_constraint(x, pltpu.HBM)

    def pairs(k):
        return [dma((n_feat,))] * k

    tiles, listed, h, ost, gst = pl.pallas_call(
        functools.partial(forward_kernel, 1.0 / float(nodes * n_node) ** 0.5),
        out_shape=(
            shape((n_node * slots, TILE, TILE), BF16),
            shape((8, n_node * slots), jnp.int32),
            shape(block, BF16),
            shape((n_feat, channels, span), BF16),
            shape((n_feat,) + pair, BF16),
        ),
        in_specs=[in_hbm] * 8,
        out_specs=(in_vmem,) * 5,
        scratch_shapes=[
            VMEM((n_node,) + block, BF16), VMEM(block, BF16),
            VMEM((row_tiles, 2 * rows, TILE), BF16), VMEM((row_tiles, 2 * rows, TILE), BF16),
            VMEM((slots * rows, TILE), F32), VMEM((row_tiles * rows, TILE), F32), VMEM(block, BF16),
            VMEM((n_feat, rows, span), BF16), VMEM((n_feat, rows, span), BF16),
            VMEM((n_feat, channels, span), BF16), VMEM((n_feat,) + pair, BF16),
            pltpu.SMEM(tile_count.shape, jnp.int32), pltpu.SMEM(tile_cols.shape, jnp.int32),
            VMEM(tile_rows.shape, jnp.int32), VMEM(tile_cols.shape, jnp.int32),
            VMEM((channels, inputs), BF16), VMEM((1, channels), F32), VMEM(pair, BF16),
            dma((8,)), dma((n_node,)), dma(()), dma((14,)), dma((14,)),
        ] + pairs(8),
        compiler_params=params(24, collective_id=0, has_side_effects=True),
        name="forward",
    )(
        keep(features), keep(tile_values.reshape(n_node * slots, TILE, TILE)), keep(cotangent),
        keep(tile_count), keep(tile_rows), keep(tile_cols),
        keep(weight.T), keep(bias.reshape(1, channels)),
    )

    acc = VMEM((row_tiles, rows, TILE), F32)
    by_tiles = VMEM((row_tiles, 2 * rows, TILE), BF16)
    scalars = [pltpu.SMEM((8, n_node * slots), jnp.int32), dma(())]
    part = pl.pallas_call(
        backward_kernel,
        out_shape=shape((n_node,) + block, BF16),
        in_specs=[in_vmem] * 3,
        out_specs=in_vmem,
        scratch_shapes=[VMEM((n_node * row_tiles, rows, TILE), F32)] + [by_tiles] * 2 + scalars,
        compiler_params=params(16),
        name="backward",
    )(listed, h, tiles)

    whole, half = VMEM(block, BF16), VMEM((rows, nodes // 2), BF16)
    fl, fr, fy, made, gwt, gb, out = pl.pallas_call(
        reduce_kernel,
        out_shape=(
            shape(block, BF16),
            shape(block, BF16),
            shape(block, BF16),
            shape((slots, rows, TILE), F32),
            shape((channels, inputs), F32),
            shape((1, channels), F32),
            shape((channels, nodes), BF16),
        ),
        in_specs=[in_smem] + [in_vmem] * 5,
        out_specs=(in_vmem,) * 7,
        scratch_shapes=[whole] * 3 + [half] * 4 + [whole] + [half] * 2 + [
            VMEM((n_feat,) + pair, BF16), VMEM((n_node,) + pair, F32),
            by_tiles, by_tiles,
            dma((14,)), dma((14,)), dma((n_node,)), dma((n_node,)),
        ] + pairs(4) + [dma(())],
        compiler_params=params(16, collective_id=1, has_side_effects=True),
        name="reduce",
    )(listed, part, h, tiles, gst, ost)

    gf, gwt, gb, out = pl.pallas_call(
        final_kernel,
        out_shape=(
            shape(block, BF16),
            shape((channels, inputs), F32),
            shape((1, channels), F32),
            shape((channels, nodes), BF16),
        ),
        in_specs=[in_vmem] * 9,
        out_specs=(in_vmem,) * 3 + (in_hbm,),
        scratch_shapes=[acc] + scalars + [dma(())],
        compiler_params=params(16),
        name="final",
    )(listed, h, fl, fr, fy, made, gwt, gb, out)
    return out, gf, gwt.T, gb.reshape(channels)


def solution(mesh):
    return jax.shard_map(
        local,
        mesh=mesh,
        in_specs=(
            P("feat", "node"),
            P(None, "feat"),
            P("feat"),
            P("node", None, None, None, None),
            P("node", None, None),
            P("node", None, None),
            P("node", None),
            P("feat", "node"),
        ),
        out_specs=(P("feat", "node"), P("feat", "node"), P(None, "feat"), P("feat")),
        check_vma=False,
    )
```

```python
import functools

import jax
import jax.numpy as jnp
from jax import lax
from jax.experimental import pallas as pl
from jax.experimental.pallas import tpu as pltpu
from jax.sharding import PartitionSpec as P

MESH = pl.DeviceIdType.MESH
VMEM = pltpu.VMEM
BF16 = jnp.bfloat16
F32 = jnp.float32
TILE = 128
GROUP = 48


def around():
    n, f = lax.axis_index("node"), lax.axis_index("feat")
    nx = lax.axis_size("node") // 2
    x, y = lax.rem(n, nx), n // nx

    def at(dx, dy):
        return (lax.rem(y + dy, 2)) * nx + lax.rem(x + dx + nx, nx)

    return n, f, at


def remote(src, dst, send, recv, node, feat):
    return pltpu.make_async_remote_copy(
        src_ref=src, dst_ref=dst, send_sem=send, recv_sem=recv, device_id=(node, feat), device_id_type=MESH
    )


def greet(places):
    barrier = pltpu.get_barrier_semaphore()
    for place in places:
        pl.semaphore_signal(barrier, inc=1, device_id=place, device_id_type=MESH)


def met(places):
    pl.semaphore_wait(pltpu.get_barrier_semaphore(), len(places))


def lanes(t, width):
    return pl.ds(pl.multiple_of(t * width, width), width)


class Sender:
    def __init__(self):
        self.sent = []

    def push(self, src, dst, send, recv, node, feat):
        self.sent.append(remote(src, dst, send, recv, node, feat))
        self.sent[-1].start()

    def arrived(self, dst, send, recv):
        remote(dst, dst, send, recv, lax.axis_index("node"), lax.axis_index("feat")).wait_recv()

    def finish(self):
        for copy in self.sent:
            copy.wait_send()


def ring(f, n_feat):
    if n_feat != 16:
        return [(d, lax.rem(f + d, n_feat), lax.rem(f - d + n_feat, n_feat)) for d in range(1, n_feat)]
    z, y, core = f // 4, lax.rem(f // 2, 2), lax.rem(f, 2)

    def by(dz, dy, dc):
        return lax.rem(z + dz + 4, 4) * 4 + lax.rem(y + dy, 2) * 2 + lax.rem(core + dc, 2)

    offsets = [(dz, dy, dc) for dz in (2, 1, 3, 0) for dy in (1, 0) for dc in (1, 0)][:-1]
    offsets.sort(key=lambda d: -(min(d[0], 4 - d[0]) + 2 * d[1] + d[2]))
    return [(dz * 4 + dy * 2 + dc, by(dz, dy, dc), by(-dz, dy, dc)) for dz, dy, dc in offsets]


def split(x):
    high = x.astype(BF16).astype(F32)
    mid = (x - high).astype(BF16).astype(F32)
    lane = lax.broadcasted_iota(jnp.int32, x.shape, 1)
    rest = jnp.where(lane == 1, mid, jnp.where(lane == 2, x - high - mid, 0.0))
    return jnp.where(lane == 0, high, rest).astype(BF16)


def by_tile(x_ref, upper, lower):
    rows = x_ref.shape[0]
    none = jnp.zeros((rows, TILE), F32)
    for t in range(upper.shape[0]):
        x = x_ref[:, t * TILE:(t + 1) * TILE].astype(F32)
        upper[t] = jnp.concatenate([x, none], axis=0).astype(BF16)
        lower[t] = jnp.concatenate([none, x], axis=0).astype(BF16)


def two(x, y, a, b, across):
    pair = jnp.concatenate([x, y], axis=1)
    both = jnp.concatenate([a, b], axis=across)
    return lax.dot_general(pair, both, (((1,), (across,)), ((), ())), preferred_element_type=F32)


def products(upper, lower, index, j, tiles, out_ref, across):
    rows = upper.shape[1] // 2
    slots = out_ref.shape[0] // rows

    @pl.loop(0, slots // GROUP)
    def _(c):
        for u in range(0, GROUP, 2):
            k = c * GROUP + u
            out_ref[pl.ds(pl.multiple_of(k * rows, rows), 2 * rows)] = two(
                upper[index[0, j, k]], lower[index[0, j, k + 1]],
                tiles[j * slots + k], tiles[j * slots + k + 1], across,
            )


def sum_tiles(count, index, j, made, out_ref, add):
    slots = index.shape[2]
    rows = made.shape[0] // slots
    row_tiles = out_ref.shape[0] // rows
    t = lax.broadcasted_iota(jnp.int32, (row_tiles, slots), 0)
    k = lax.broadcasted_iota(jnp.int32, (row_tiles, slots), 1)
    hit = jnp.where((t == index[0, pl.ds(j, 1)]) & (k < count[0, j]), 1.0, 0.0).astype(BF16)
    for c in range(rows):
        part = made[pl.ds(c, slots, stride=rows), :]
        high = part.astype(BF16)
        low = (part - high.astype(F32)).astype(BF16)
        where = pl.ds(c, row_tiles, stride=rows)
        total = jnp.dot(hit, high, preferred_element_type=F32) + jnp.dot(hit, low, preferred_element_type=F32)
        out_ref[where, :] = out_ref[where, :] + total if add else total


def layer_kernel(
    norm, x_ref, tiles_ref, cot_ref, count_ref, rows_ref, cols_ref, wt_ref, bias_ref,
    own_sum, fl_in, fr_in, fy_in, gw_out, gb_out, out_ref,
    tiles, x_all, x_own, upper, lower, made, tile_sum, z_ref, zin, hst, cin, win, h_ref, ost, gst,
    part_ref, far_in, dl_in, dr_in, hl_in, hr_in, hl_out, hr_out, y_out, r_out, l_out, gin, gall,
    count, rows_at, cols_at, rows_in, cols_in, wt_in, bias_in, wst,
    local_sem, tile_sem, own_sem, send, recv, back_send, back_recv, s_send, s_recv,
    c_send, c_recv, w_send, w_recv, z_send, z_recv, h_send, h_recv, g_send, g_recv, o_send, o_recv,
):
    n, f, at = around()
    n_feat, channels, span = cin.shape
    rows = x_ref.shape[0]
    inputs = wt_ref.shape[1]
    hidden = n_feat * channels
    n_node = count_ref.shape[1]
    slots = tiles.shape[0] // n_node
    half = x_ref.shape[1] // 2
    right, left, other, far = at(1, 0), at(-1, 0), at(0, 1), at(2, 0)
    order = [n, left, right, other, far, at(-1, 1), at(1, 1), at(2, 1)]
    link = Sender()
    here = [
        pltpu.make_async_copy(src, dst, local_sem.at[i])
        for i, (src, dst) in enumerate([
            (wt_ref, wt_in), (bias_ref, bias_in), (count_ref, count), (rows_ref, rows_in), (cols_ref, cols_in),
            (rows_ref, rows_at), (cols_ref, cols_at), (x_ref, x_own), (cot_ref.at[:, lanes(f, span)], cin.at[f]),
        ])
    ]
    moved = [
        pltpu.make_async_copy(
            tiles_ref.at[pl.ds(j * slots, slots)], tiles.at[pl.ds(j * slots, slots)], tile_sem.at[s]
        )
        for s, j in enumerate(order)
    ]
    partners = ring(f, n_feat)
    places = [(lax.rem(n + d, n_node), f) for d in range(1, n_node)] + [(n, p) for _, p, _ in partners]
    greet(places)
    for copy in here:
        copy.start()
    met(places)

    low, high = pl.ds(0, half), pl.ds(half, half)

    def push(m, part, k, to, src=None):
        block = x_all.at[m, :, part]
        link.push(block if src is None else src.at[:, part], block, send.at[k], recv.at[k], to, f)

    def arrived(m, part, k):
        link.arrived(x_all.at[m, :, part], send.at[k], recv.at[k])

    def work(s):
        moved[s].wait()
        by_tile(x_own if s == 0 else x_all.at[order[s]], upper, lower)
        products(upper, lower, cols_at, order[s], tiles, made, 1)
        sum_tiles(count, rows_in, order[s], made, tile_sum, True)

    push(n, low, 0, right, x_ref)
    push(n, high, 1, left, x_ref)
    push(n, low, 2, other, x_ref)
    push(n, high, 3, right, x_ref)
    push(n, low, 4, left, x_ref)
    push(n, high, 5, other, x_ref)
    for d, p, _ in partners:
        link.push(cot_ref.at[:, lanes(p, span)], cin.at[f], c_send.at[d], c_recv.at[d], n, p)
    for copy in here[:2]:
        copy.wait()
    wst[0] = wt_in[...]
    wst[1] = split(jnp.broadcast_to(bias_in[...], (inputs, channels)).T)
    win[f] = wst[...]
    for d, p, _ in partners:
        link.push(wst, win.at[f], w_send.at[d], w_recv.at[d], n, p)
    for copy in moved:
        copy.start()
    for copy in here[2:]:
        copy.wait()
    for t in range(upper.shape[0]):
        tile_sum[t * rows:(t + 1) * rows] = x_own[:, t * TILE:(t + 1) * TILE].astype(F32)
    work(0)
    arrived(left, low, 0)
    push(left, low, 6, right)
    arrived(right, high, 1)
    push(right, high, 7, left)
    arrived(other, low, 2)
    push(other, low, 8, right)
    push(other, low, 9, left)
    arrived(other, high, 5)
    push(other, high, 10, right)
    push(other, high, 11, left)
    arrived(left, high, 3)
    work(1)
    arrived(far, low, 6)
    push(far, low, 12, other)
    arrived(far, high, 7)
    push(far, high, 13, other)
    arrived(right, low, 4)
    work(2)
    work(3)
    work(4)
    arrived(at(-1, 1), low, 8)
    arrived(at(-1, 1), high, 10)
    work(5)
    arrived(at(1, 1), low, 9)
    arrived(at(1, 1), high, 11)
    work(6)
    arrived(at(2, 1), low, 12)
    arrived(at(2, 1), high, 13)
    work(7)
    for t in range(upper.shape[0]):
        z_ref[:, t * TILE:(t + 1) * TILE] = tile_sum[t * rows:(t + 1) * rows].astype(BF16)
    for d, p, _ in partners:
        link.push(z_ref.at[:, lanes(p, span)], zin.at[f], z_send.at[d], z_recv.at[d], n, p)
    zin[f] = z_ref[:, lanes(f, span)]
    for d, _, p in partners:
        link.arrived(cin.at[p], c_send.at[d], c_recv.at[d])
        link.arrived(win.at[p], w_send.at[d], w_recv.at[d])
    wt = win[:, 0].reshape(hidden, inputs)
    bias = jnp.sum(win[:, 1].reshape(hidden, inputs).astype(F32), axis=1, keepdims=True)
    cot = cin[...].reshape(hidden, span)
    w = wt.astype(F32).T.astype(BF16)
    for d, _, p in partners:
        link.arrived(zin.at[p], z_send.at[d], z_recv.at[d])
    z = zin[...].astype(F32).reshape(n_feat * rows, span).astype(BF16)
    parts = []
    for t in range(span // TILE):
        part = slice(t * TILE, (t + 1) * TILE)
        pre = jnp.dot(wt, z[:, part], preferred_element_type=F32) + bias
        s = jax.nn.sigmoid(pre)
        g = (cot[:, part].astype(F32) * s * (1.0 + pre * (1.0 - s))).astype(BF16)
        h = jnp.dot(w, g, preferred_element_type=F32)
        hst[:, :, part] = h.reshape(n_feat, rows, TILE).astype(BF16)
        ost[:, :, part] = (pre * s).astype(BF16).reshape(n_feat, channels, TILE)
        parts.append(g)
    for d, p, _ in partners:
        link.push(hst.at[p], h_ref.at[:, lanes(f, span)], h_send.at[d], h_recv.at[d], n, p)
    own_h = pltpu.make_async_copy(hst.at[f], h_ref.at[:, lanes(f, span)], own_sem.at[0])
    own_h.start()
    g = jnp.concatenate(parts, axis=1)
    both = jnp.concatenate([z, jnp.ones_like(z)], axis=0)
    sums = lax.dot_general(g, both, (((1,), (1,)), ((), ())), preferred_element_type=F32) * norm
    gst[:, 0] = sums[:, :inputs].astype(BF16).reshape(n_feat, channels, inputs)
    gst[:, 1] = split(sums[:, inputs:]).reshape(n_feat, channels, inputs)
    for d, p, _ in partners:
        link.push(gst.at[p], gin.at[f], g_send.at[d], g_recv.at[d], n, p)
    gin[f] = gst[f]
    for d, p, _ in partners:
        link.push(ost.at[p], out_ref.at[:, lanes(f, span)], o_send.at[d], o_recv.at[d], n, p)
    own_out = pltpu.make_async_copy(ost.at[f], out_ref.at[:, lanes(f, span)], own_sem.at[1])
    own_out.start()
    for d, _, p in partners:
        link.arrived(h_ref.at[:, lanes(p, span)], h_send.at[d], h_recv.at[d])
    own_h.wait()

    def go(src, dst, k, to):
        link.push(src, dst, back_send.at[k], back_recv.at[k], to, f)

    def came(dst, k):
        link.arrived(dst, back_send.at[k], back_recv.at[k])

    def add(*terms):
        total = terms[0].astype(F32)
        for term in terms[1:]:
            total = total + term.astype(F32)
        return total.astype(BF16)

    def spread(j):
        products(upper, lower, rows_at, j, tiles, made, 0)
        sum_tiles(count, cols_in, j, made, tile_sum, False)
        for t in range(upper.shape[0]):
            part_ref[j, :, t * TILE:(t + 1) * TILE] = tile_sum[t * rows:(t + 1) * rows].astype(BF16)

    halves = (low, high)
    by_tile(h_ref, upper, lower)
    spread(at(2, 1))
    for i, part in enumerate(halves):
        go(part_ref.at[at(2, 1), :, part], far_in.at[:, part], i, other)
    spread(at(1, 1))
    for i, part in enumerate(halves):
        go(part_ref.at[at(1, 1), :, part], dl_in.at[:, part], 2 + i, right)
    spread(at(-1, 1))
    for i, part in enumerate(halves):
        go(part_ref.at[at(-1, 1), :, part], dr_in.at[:, part], 4 + i, left)
    spread(far)
    came(far_in.at[:, low], 0)
    hl_out[...] = add(part_ref[far, :, low], far_in[:, low])
    go(hl_out, hl_in, 6, right)
    came(far_in.at[:, high], 1)
    hr_out[...] = add(part_ref[far, :, high], far_in[:, high])
    go(hr_out, hr_in, 7, left)
    spread(other)
    came(dl_in.at[:, low], 2)
    came(dr_in.at[:, low], 4)
    y_out[:, low] = add(part_ref[other, :, low], dl_in[:, low], dr_in[:, low])
    go(y_out.at[:, low], fy_in.at[:, low], 10, other)
    spread(right)
    go(part_ref.at[right, :, high], fl_in.at[:, high], 8, right)
    came(dl_in.at[:, high], 3)
    came(dr_in.at[:, high], 5)
    y_out[:, high] = add(part_ref[other, :, high], dl_in[:, high], dr_in[:, high])
    go(y_out.at[:, high], fy_in.at[:, high], 11, other)
    spread(left)
    go(part_ref.at[left, :, low], fr_in.at[:, low], 9, left)
    for d, _, p in partners:
        link.arrived(gin.at[p], g_send.at[d], g_recv.at[d])
    gall[n] = jnp.sum(gin[...].astype(F32), axis=0)
    for d in range(1, n_node):
        link.push(gall.at[n], gall.at[n], s_send.at[d], s_recv.at[d], lax.rem(n + d, n_node), f)
    came(hl_in, 6)
    r_out[...] = add(part_ref[right, :, low], hl_in[...])
    go(r_out, fl_in.at[:, low], 12, right)
    came(hr_in, 7)
    l_out[...] = add(part_ref[left, :, high], hr_in[...])
    go(l_out, fr_in.at[:, high], 13, left)
    for t in range(upper.shape[0]):
        own_sum[t * rows:(t + 1) * rows] = h_ref[:, t * TILE:(t + 1) * TILE].astype(F32)
    products(upper, lower, rows_at, n, tiles, made, 0)
    sum_tiles(count, cols_in, n, made, own_sum, True)
    for d in range(1, n_node):
        link.arrived(gall.at[lax.rem(n - d + n_node, n_node)], s_send.at[d], s_recv.at[d])
    total = jnp.sum(gall[...], axis=0)
    gw_out[...] = total[0]
    gb_out[...] = jnp.sum(total[1].T, axis=0, keepdims=True)
    for d, _, p in partners:
        link.arrived(out_ref.at[:, lanes(p, span)], o_send.at[d], o_recv.at[d])
    own_out.wait()
    came(fl_in.at[:, high], 8)
    came(fr_in.at[:, low], 9)
    for i, part in enumerate(halves):
        came(fy_in.at[:, part], 10 + i)
    came(fl_in.at[:, low], 12)
    came(fr_in.at[:, high], 13)
    link.finish()


def final_kernel(
    own_sum, fl, fr, fy, gw_ref, gb_ref, made_out,
    gf_ref, gw_out, gb_out, out_ref, out_sem,
):
    moved = pltpu.make_async_copy(made_out, out_ref, out_sem)
    moved.start()
    rows = gf_ref.shape[0]
    for t in range(gf_ref.shape[1] // TILE):
        span = slice(t * TILE, (t + 1) * TILE)
        gf_ref[:, span] = (
            own_sum[t * rows:(t + 1) * rows] + fl[:, span].astype(F32)
            + fr[:, span].astype(F32) + fy[:, span].astype(F32)
        ).astype(BF16)
    gw_out[...] = gw_ref[...]
    gb_out[...] = gb_ref[...]
    moved.wait()


def local(features, weight, bias, tile_values, tile_rows, tile_cols, tile_count, cotangent):
    n_node, n_feat = lax.axis_size("node"), lax.axis_size("feat")
    rows, nodes = features.shape
    inputs, channels = weight.shape
    row_tiles = nodes // TILE
    span = row_tiles // n_feat * TILE
    slots = tile_rows.shape[2]
    dma = pltpu.SemaphoreType.DMA
    in_vmem = pl.BlockSpec(memory_space=VMEM)
    in_smem = pl.BlockSpec(memory_space=pltpu.SMEM)
    in_hbm = pl.BlockSpec(memory_space=pltpu.HBM)
    shape = jax.ShapeDtypeStruct
    block = (rows, nodes)
    pair = (2, channels, inputs)

    def params(mib, **more):
        return pltpu.CompilerParams(vmem_limit_bytes=mib << 20, **more)

    def keep(x):
        return pltpu.with_memory_space_constraint(x, pltpu.HBM)

    def pairs(k):
        return [dma((n_feat,))] * k

    by_tiles = VMEM((row_tiles, 2 * rows, TILE), BF16)
    whole, half = VMEM(block, BF16), VMEM((rows, nodes // 2), BF16)
    sums = (row_tiles * rows, TILE)
    own, fl, fr, fy, gwt, gb, out = pl.pallas_call(
        functools.partial(layer_kernel, 1.0 / float(nodes * n_node) ** 0.5),
        out_shape=(
            shape(sums, F32),
            shape(block, BF16),
            shape(block, BF16),
            shape(block, BF16),
            shape((channels, inputs), F32),
            shape((1, channels), F32),
            shape((channels, nodes), BF16),
        ),
        in_specs=[in_hbm] * 8,
        out_specs=(in_vmem,) * 7,
        scratch_shapes=[
            VMEM((n_node * slots, TILE, TILE), BF16), VMEM((n_node,) + block, BF16), whole,
            by_tiles, by_tiles, VMEM((slots * rows, TILE), F32), VMEM(sums, F32), whole,
            VMEM((n_feat, rows, span), BF16), VMEM((n_feat, rows, span), BF16),
            VMEM((n_feat, channels, span), BF16), VMEM((n_feat,) + pair, BF16), whole,
            VMEM((n_feat, channels, span), BF16), VMEM((n_feat,) + pair, BF16),
            VMEM((n_node,) + block, BF16), whole, whole, whole, half, half, half, half, whole, half, half,
            VMEM((n_feat,) + pair, BF16), VMEM((n_node,) + pair, F32),
            pltpu.SMEM(tile_count.shape, jnp.int32), pltpu.SMEM(tile_rows.shape, jnp.int32),
            pltpu.SMEM(tile_cols.shape, jnp.int32),
            VMEM(tile_rows.shape, jnp.int32), VMEM(tile_cols.shape, jnp.int32),
            VMEM((channels, inputs), BF16), VMEM((1, channels), F32), VMEM(pair, BF16),
            dma((9,)), dma((n_node,)), dma((2,)), dma((14,)), dma((14,)), dma((14,)), dma((14,)),
            dma((n_node,)), dma((n_node,)),
        ] + pairs(12),
        compiler_params=params(40, collective_id=0, has_side_effects=True),
        name="layer",
    )(
        keep(features), keep(tile_values.reshape(n_node * slots, TILE, TILE)), keep(cotangent),
        keep(tile_count), keep(tile_rows), keep(tile_cols),
        keep(weight.T), keep(bias.reshape(1, channels)),
    )

    gf, gwt, gb, out = pl.pallas_call(
        final_kernel,
        out_shape=(
            shape(block, BF16),
            shape((channels, inputs), F32),
            shape((1, channels), F32),
            shape((channels, nodes), BF16),
        ),
        in_specs=[in_vmem] * 7,
        out_specs=(in_vmem,) * 3 + (in_hbm,),
        scratch_shapes=[dma(())],
        compiler_params=params(16),
        name="final",
    )(own, fl, fr, fy, gwt, gb, out)
    return out, gf, gwt.T, gb.reshape(channels)


def solution(mesh):
    return jax.shard_map(
        local,
        mesh=mesh,
        in_specs=(
            P("feat", "node"),
            P(None, "feat"),
            P("feat"),
            P("node", None, None, None, None),
            P("node", None, None),
            P("node", None, None),
            P("node", None),
            P("feat", "node"),
        ),
        out_specs=(P("feat", "node"), P("feat", "node"), P(None, "feat"), P("feat")),
        check_vma=False,
    )
```

```python
import functools

import jax
import jax.numpy as jnp
from jax import lax
from jax.experimental import pallas as pl
from jax.experimental.pallas import tpu as pltpu
from jax.sharding import PartitionSpec as P

MESH = pl.DeviceIdType.MESH
VMEM = pltpu.VMEM
BF16 = jnp.bfloat16
F32 = jnp.float32
TILE = 128
GROUP = 48


def around():
    n, f = lax.axis_index("node"), lax.axis_index("feat")
    nx = lax.axis_size("node") // 2
    x, y = lax.rem(n, nx), n // nx

    def at(dx, dy):
        return (lax.rem(y + dy, 2)) * nx + lax.rem(x + dx + nx, nx)

    return n, f, at


def remote(src, dst, send, recv, node, feat):
    return pltpu.make_async_remote_copy(
        src_ref=src, dst_ref=dst, send_sem=send, recv_sem=recv, device_id=(node, feat), device_id_type=MESH
    )


def greet(places):
    barrier = pltpu.get_barrier_semaphore()
    for place in places:
        pl.semaphore_signal(barrier, inc=1, device_id=place, device_id_type=MESH)


def met(places):
    pl.semaphore_wait(pltpu.get_barrier_semaphore(), len(places))


def lanes(t, width):
    return pl.ds(pl.multiple_of(t * width, width), width)


class Sender:
    def __init__(self):
        self.sent = []

    def push(self, src, dst, send, recv, node, feat):
        self.sent.append(remote(src, dst, send, recv, node, feat))
        self.sent[-1].start()

    def arrived(self, dst, send, recv):
        remote(dst, dst, send, recv, lax.axis_index("node"), lax.axis_index("feat")).wait_recv()

    def finish(self):
        for copy in self.sent:
            copy.wait_send()


def ring(f, n_feat):
    if n_feat != 16:
        return [(d, lax.rem(f + d, n_feat), lax.rem(f - d + n_feat, n_feat)) for d in range(1, n_feat)]
    z, y, core = f // 4, lax.rem(f // 2, 2), lax.rem(f, 2)

    def by(dz, dy, dc):
        return lax.rem(z + dz + 4, 4) * 4 + lax.rem(y + dy, 2) * 2 + lax.rem(core + dc, 2)

    offsets = [(dz, dy, dc) for dz in (2, 1, 3, 0) for dy in (1, 0) for dc in (1, 0)][:-1]
    offsets.sort(key=lambda d: -(min(d[0], 4 - d[0]) + 2 * d[1] + d[2]))
    return [(dz * 4 + dy * 2 + dc, by(dz, dy, dc), by(-dz, dy, dc)) for dz, dy, dc in offsets]


def split(x):
    high = x.astype(BF16).astype(F32)
    mid = (x - high).astype(BF16).astype(F32)
    lane = lax.broadcasted_iota(jnp.int32, x.shape, 1)
    rest = jnp.where(lane == 1, mid, jnp.where(lane == 2, x - high - mid, 0.0))
    return jnp.where(lane == 0, high, rest).astype(BF16)


def by_tile(x_ref, upper, lower):
    rows = x_ref.shape[0]
    none = jnp.zeros((rows, TILE), F32)
    for t in range(upper.shape[0]):
        x = x_ref[:, t * TILE:(t + 1) * TILE].astype(F32)
        upper[t] = jnp.concatenate([x, none], axis=0).astype(BF16)
        lower[t] = jnp.concatenate([none, x], axis=0).astype(BF16)


def two(x, y, a, b, across):
    pair = jnp.concatenate([x, y], axis=1)
    both = jnp.concatenate([a, b], axis=across)
    return lax.dot_general(pair, both, (((1,), (across,)), ((), ())), preferred_element_type=F32)


def products(upper, lower, index, j, tiles, out_ref, across):
    rows = upper.shape[1] // 2
    slots = out_ref.shape[0] // rows

    @pl.loop(0, slots // GROUP)
    def _(c):
        for u in range(0, GROUP, 2):
            k = c * GROUP + u
            out_ref[pl.ds(pl.multiple_of(k * rows, rows), 2 * rows)] = two(
                upper[index[0, j, k]], lower[index[0, j, k + 1]],
                tiles[j * slots + k], tiles[j * slots + k + 1], across,
            )


def sum_tiles(count, index, j, made, out_ref, add):
    slots = index.shape[2]
    rows = made.shape[0] // slots
    row_tiles = out_ref.shape[0] // rows
    t = lax.broadcasted_iota(jnp.int32, (row_tiles, slots), 0)
    k = lax.broadcasted_iota(jnp.int32, (row_tiles, slots), 1)
    hit = jnp.where((t == index[0, pl.ds(j, 1)]) & (k < count[0, j]), 1.0, 0.0).astype(BF16)
    for c in range(rows):
        part = made[pl.ds(c, slots, stride=rows), :]
        high = part.astype(BF16)
        low = (part - high.astype(F32)).astype(BF16)
        where = pl.ds(c, row_tiles, stride=rows)
        total = jnp.dot(hit, jnp.concatenate([high, low], axis=1), preferred_element_type=F32)
        total = total[:, :TILE] + total[:, TILE:]
        out_ref[where, :] = out_ref[where, :] + total if add else total


def layer_kernel(
    norm, x_ref, tiles_ref, cot_ref, count_ref, rows_ref, cols_ref, wt_ref, bias_ref,
    own_sum, fl_in, fr_in, fy_in, gw_out, gb_out, out_ref,
    tiles, x_all, x_own, upper, lower, made, tile_sum, z_ref, zin, hst, cin, win, h_ref, ost, gst,
    part_ref, far_in, dl_in, dr_in, hl_in, hr_in, hl_out, hr_out, y_out, r_out, l_out, gin, gall,
    count, rows_at, cols_at, rows_in, cols_in, wt_in, bias_in, wst,
    local_sem, tile_sem, own_sem, send, recv, back_send, back_recv, s_send, s_recv,
    c_send, c_recv, w_send, w_recv, z_send, z_recv, h_send, h_recv, g_send, g_recv, o_send, o_recv,
):
    n, f, at = around()
    n_feat, channels, span = cin.shape
    rows = x_ref.shape[0]
    inputs = wt_ref.shape[1]
    hidden = n_feat * channels
    n_node = count_ref.shape[1]
    slots = tiles.shape[0] // n_node
    half = x_ref.shape[1] // 2
    right, left, other, far = at(1, 0), at(-1, 0), at(0, 1), at(2, 0)
    order = [n, left, right, other, far, at(-1, 1), at(1, 1), at(2, 1)]
    link = Sender()
    here = [
        pltpu.make_async_copy(src, dst, local_sem.at[i])
        for i, (src, dst) in enumerate([
            (wt_ref, wt_in), (bias_ref, bias_in), (count_ref, count), (rows_ref, rows_in), (cols_ref, cols_in),
            (rows_ref, rows_at), (cols_ref, cols_at), (x_ref, x_own), (cot_ref.at[:, lanes(f, span)], cin.at[f]),
        ])
    ]
    moved = [
        pltpu.make_async_copy(
            tiles_ref.at[pl.ds(j * slots, slots)], tiles.at[pl.ds(j * slots, slots)], tile_sem.at[s]
        )
        for s, j in enumerate(order)
    ]
    partners = ring(f, n_feat)
    places = [(lax.rem(n + d, n_node), f) for d in range(1, n_node)] + [(n, p) for _, p, _ in partners]
    greet(places)
    for copy in here:
        copy.start()
    met(places)

    low, high = pl.ds(0, half), pl.ds(half, half)

    def push(m, part, k, to, src=None):
        block = x_all.at[m, :, part]
        link.push(block if src is None else src.at[:, part], block, send.at[k], recv.at[k], to, f)

    def arrived(m, part, k):
        link.arrived(x_all.at[m, :, part], send.at[k], recv.at[k])

    def work(s):
        moved[s].wait()
        by_tile(x_own if s == 0 else x_all.at[order[s]], upper, lower)
        products(upper, lower, cols_at, order[s], tiles, made, 1)
        sum_tiles(count, rows_in, order[s], made, tile_sum, True)

    push(n, low, 0, right, x_ref)
    push(n, high, 1, left, x_ref)
    push(n, low, 2, other, x_ref)
    push(n, high, 3, right, x_ref)
    push(n, low, 4, left, x_ref)
    push(n, high, 5, other, x_ref)
    for d, p, _ in partners:
        link.push(cot_ref.at[:, lanes(p, span)], cin.at[f], c_send.at[d], c_recv.at[d], n, p)
    for copy in here[:2]:
        copy.wait()
    wst[0] = wt_in[...]
    wst[1] = split(jnp.broadcast_to(bias_in[...], (inputs, channels)).T)
    win[f] = wst[...]
    for d, p, _ in partners:
        link.push(wst, win.at[f], w_send.at[d], w_recv.at[d], n, p)
    for copy in moved:
        copy.start()
    for copy in here[2:]:
        copy.wait()
    for t in range(upper.shape[0]):
        tile_sum[t * rows:(t + 1) * rows] = x_own[:, t * TILE:(t + 1) * TILE].astype(F32)
    work(0)
    arrived(left, low, 0)
    push(left, low, 6, right)
    arrived(right, high, 1)
    push(right, high, 7, left)
    arrived(other, low, 2)
    push(other, low, 8, right)
    push(other, low, 9, left)
    arrived(other, high, 5)
    push(other, high, 10, right)
    push(other, high, 11, left)
    arrived(left, high, 3)
    work(1)
    arrived(far, low, 6)
    push(far, low, 12, other)
    arrived(far, high, 7)
    push(far, high, 13, other)
    arrived(right, low, 4)
    work(2)
    work(3)
    work(4)
    arrived(at(-1, 1), low, 8)
    arrived(at(-1, 1), high, 10)
    work(5)
    arrived(at(1, 1), low, 9)
    arrived(at(1, 1), high, 11)
    work(6)
    arrived(at(2, 1), low, 12)
    arrived(at(2, 1), high, 13)
    work(7)
    for t in range(upper.shape[0]):
        z_ref[:, t * TILE:(t + 1) * TILE] = tile_sum[t * rows:(t + 1) * rows].astype(BF16)
    for d, p, _ in partners:
        link.push(z_ref.at[:, lanes(p, span)], zin.at[f], z_send.at[d], z_recv.at[d], n, p)
    zin[f] = z_ref[:, lanes(f, span)]
    for d, _, p in partners:
        link.arrived(cin.at[p], c_send.at[d], c_recv.at[d])
        link.arrived(win.at[p], w_send.at[d], w_recv.at[d])
    wt = win[:, 0].reshape(hidden, inputs)
    bias = jnp.sum(win[:, 1].reshape(hidden, inputs).astype(F32), axis=1, keepdims=True)
    cot = cin[...].reshape(hidden, span)
    w = wt.astype(F32).T.astype(BF16)
    for d, _, p in partners:
        link.arrived(zin.at[p], z_send.at[d], z_recv.at[d])
    z = zin[...].astype(F32).reshape(n_feat * rows, span).astype(BF16)
    parts = []
    for t in range(span // TILE):
        part = slice(t * TILE, (t + 1) * TILE)
        pre = jnp.dot(wt, z[:, part], preferred_element_type=F32) + bias
        s = jax.nn.sigmoid(pre)
        g = (cot[:, part].astype(F32) * s * (1.0 + pre * (1.0 - s))).astype(BF16)
        h = jnp.dot(w, g, preferred_element_type=F32)
        hst[:, :, part] = h.reshape(n_feat, rows, TILE).astype(BF16)
        ost[:, :, part] = (pre * s).astype(BF16).reshape(n_feat, channels, TILE)
        parts.append(g)
    for d, p, _ in partners:
        link.push(hst.at[p], h_ref.at[:, lanes(f, span)], h_send.at[d], h_recv.at[d], n, p)
    own_h = pltpu.make_async_copy(hst.at[f], h_ref.at[:, lanes(f, span)], own_sem.at[0])
    own_h.start()
    g = jnp.concatenate(parts, axis=1)
    both = jnp.concatenate([z, jnp.ones_like(z)], axis=0)
    sums = lax.dot_general(g, both, (((1,), (1,)), ((), ())), preferred_element_type=F32) * norm
    gst[:, 0] = sums[:, :inputs].astype(BF16).reshape(n_feat, channels, inputs)
    gst[:, 1] = split(sums[:, inputs:]).reshape(n_feat, channels, inputs)
    for d, p, _ in partners:
        link.push(gst.at[p], gin.at[f], g_send.at[d], g_recv.at[d], n, p)
    gin[f] = gst[f]
    for d, p, _ in partners:
        link.push(ost.at[p], out_ref.at[:, lanes(f, span)], o_send.at[d], o_recv.at[d], n, p)
    own_out = pltpu.make_async_copy(ost.at[f], out_ref.at[:, lanes(f, span)], own_sem.at[1])
    own_out.start()
    for d, _, p in partners:
        link.arrived(h_ref.at[:, lanes(p, span)], h_send.at[d], h_recv.at[d])
    own_h.wait()

    def go(src, dst, k, to):
        link.push(src, dst, back_send.at[k], back_recv.at[k], to, f)

    def came(dst, k):
        link.arrived(dst, back_send.at[k], back_recv.at[k])

    def add(*terms):
        total = terms[0].astype(F32)
        for term in terms[1:]:
            total = total + term.astype(F32)
        return total.astype(BF16)

    def spread(j):
        products(upper, lower, rows_at, j, tiles, made, 0)
        sum_tiles(count, cols_in, j, made, tile_sum, False)
        for t in range(upper.shape[0]):
            part_ref[j, :, t * TILE:(t + 1) * TILE] = tile_sum[t * rows:(t + 1) * rows].astype(BF16)

    halves = (low, high)
    by_tile(h_ref, upper, lower)
    spread(at(2, 1))
    for i, part in enumerate(halves):
        go(part_ref.at[at(2, 1), :, part], far_in.at[:, part], i, other)
    spread(at(1, 1))
    for i, part in enumerate(halves):
        go(part_ref.at[at(1, 1), :, part], dl_in.at[:, part], 2 + i, right)
    spread(at(-1, 1))
    for i, part in enumerate(halves):
        go(part_ref.at[at(-1, 1), :, part], dr_in.at[:, part], 4 + i, left)
    spread(far)
    came(far_in.at[:, low], 0)
    hl_out[...] = add(part_ref[far, :, low], far_in[:, low])
    go(hl_out, hl_in, 6, right)
    came(far_in.at[:, high], 1)
    hr_out[...] = add(part_ref[far, :, high], far_in[:, high])
    go(hr_out, hr_in, 7, left)
    spread(other)
    came(dl_in.at[:, low], 2)
    came(dr_in.at[:, low], 4)
    y_out[:, low] = add(part_ref[other, :, low], dl_in[:, low], dr_in[:, low])
    go(y_out.at[:, low], fy_in.at[:, low], 10, other)
    spread(right)
    go(part_ref.at[right, :, high], fl_in.at[:, high], 8, right)
    came(dl_in.at[:, high], 3)
    came(dr_in.at[:, high], 5)
    y_out[:, high] = add(part_ref[other, :, high], dl_in[:, high], dr_in[:, high])
    go(y_out.at[:, high], fy_in.at[:, high], 11, other)
    spread(left)
    go(part_ref.at[left, :, low], fr_in.at[:, low], 9, left)
    for d, _, p in partners:
        link.arrived(gin.at[p], g_send.at[d], g_recv.at[d])
    gall[n] = jnp.sum(gin[...].astype(F32), axis=0)
    for d in range(1, n_node):
        link.push(gall.at[n], gall.at[n], s_send.at[d], s_recv.at[d], lax.rem(n + d, n_node), f)
    came(hl_in, 6)
    r_out[...] = add(part_ref[right, :, low], hl_in[...])
    go(r_out, fl_in.at[:, low], 12, right)
    came(hr_in, 7)
    l_out[...] = add(part_ref[left, :, high], hr_in[...])
    go(l_out, fr_in.at[:, high], 13, left)
    for t in range(upper.shape[0]):
        own_sum[t * rows:(t + 1) * rows] = h_ref[:, t * TILE:(t + 1) * TILE].astype(F32)
    products(upper, lower, rows_at, n, tiles, made, 0)
    sum_tiles(count, cols_in, n, made, own_sum, True)
    for d in range(1, n_node):
        link.arrived(gall.at[lax.rem(n - d + n_node, n_node)], s_send.at[d], s_recv.at[d])
    total = jnp.sum(gall[...], axis=0)
    gw_out[...] = total[0]
    gb_out[...] = jnp.sum(total[1].T, axis=0, keepdims=True)
    for d, _, p in partners:
        link.arrived(out_ref.at[:, lanes(p, span)], o_send.at[d], o_recv.at[d])
    own_out.wait()
    came(fl_in.at[:, high], 8)
    came(fr_in.at[:, low], 9)
    for i, part in enumerate(halves):
        came(fy_in.at[:, part], 10 + i)
    came(fl_in.at[:, low], 12)
    came(fr_in.at[:, high], 13)
    link.finish()


def final_kernel(
    own_sum, fl, fr, fy, gw_ref, gb_ref, made_out,
    gf_ref, gw_out, gb_out, out_ref, out_sem,
):
    moved = pltpu.make_async_copy(made_out, out_ref, out_sem)
    moved.start()
    rows = gf_ref.shape[0]
    for t in range(gf_ref.shape[1] // TILE):
        span = slice(t * TILE, (t + 1) * TILE)
        gf_ref[:, span] = (
            own_sum[t * rows:(t + 1) * rows] + fl[:, span].astype(F32)
            + fr[:, span].astype(F32) + fy[:, span].astype(F32)
        ).astype(BF16)
    gw_out[...] = gw_ref[...]
    gb_out[...] = gb_ref[...]
    moved.wait()


def local(features, weight, bias, tile_values, tile_rows, tile_cols, tile_count, cotangent):
    n_node, n_feat = lax.axis_size("node"), lax.axis_size("feat")
    rows, nodes = features.shape
    inputs, channels = weight.shape
    row_tiles = nodes // TILE
    span = row_tiles // n_feat * TILE
    slots = tile_rows.shape[2]
    dma = pltpu.SemaphoreType.DMA
    in_vmem = pl.BlockSpec(memory_space=VMEM)
    in_smem = pl.BlockSpec(memory_space=pltpu.SMEM)
    in_hbm = pl.BlockSpec(memory_space=pltpu.HBM)
    shape = jax.ShapeDtypeStruct
    block = (rows, nodes)
    pair = (2, channels, inputs)

    def params(mib, **more):
        return pltpu.CompilerParams(vmem_limit_bytes=mib << 20, **more)

    def keep(x):
        return pltpu.with_memory_space_constraint(x, pltpu.HBM)

    def pairs(k):
        return [dma((n_feat,))] * k

    by_tiles = VMEM((row_tiles, 2 * rows, TILE), BF16)
    whole, half = VMEM(block, BF16), VMEM((rows, nodes // 2), BF16)
    sums = (row_tiles * rows, TILE)
    own, fl, fr, fy, gwt, gb, out = pl.pallas_call(
        functools.partial(layer_kernel, 1.0 / float(nodes * n_node) ** 0.5),
        out_shape=(
            shape(sums, F32),
            shape(block, BF16),
            shape(block, BF16),
            shape(block, BF16),
            shape((channels, inputs), F32),
            shape((1, channels), F32),
            shape((channels, nodes), BF16),
        ),
        in_specs=[in_hbm] * 8,
        out_specs=(in_vmem,) * 7,
        scratch_shapes=[
            VMEM((n_node * slots, TILE, TILE), BF16), VMEM((n_node,) + block, BF16), whole,
            by_tiles, by_tiles, VMEM((slots * rows, TILE), F32), VMEM(sums, F32), whole,
            VMEM((n_feat, rows, span), BF16), VMEM((n_feat, rows, span), BF16),
            VMEM((n_feat, channels, span), BF16), VMEM((n_feat,) + pair, BF16), whole,
            VMEM((n_feat, channels, span), BF16), VMEM((n_feat,) + pair, BF16),
            VMEM((n_node,) + block, BF16), whole, whole, whole, half, half, half, half, whole, half, half,
            VMEM((n_feat,) + pair, BF16), VMEM((n_node,) + pair, F32),
            pltpu.SMEM(tile_count.shape, jnp.int32), pltpu.SMEM(tile_rows.shape, jnp.int32),
            pltpu.SMEM(tile_cols.shape, jnp.int32),
            VMEM(tile_rows.shape, jnp.int32), VMEM(tile_cols.shape, jnp.int32),
            VMEM((channels, inputs), BF16), VMEM((1, channels), F32), VMEM(pair, BF16),
            dma((9,)), dma((n_node,)), dma((2,)), dma((14,)), dma((14,)), dma((14,)), dma((14,)),
            dma((n_node,)), dma((n_node,)),
        ] + pairs(12),
        compiler_params=params(40, collective_id=0, has_side_effects=True),
        name="layer",
    )(
        keep(features), keep(tile_values.reshape(n_node * slots, TILE, TILE)), keep(cotangent),
        keep(tile_count), keep(tile_rows), keep(tile_cols),
        keep(weight.T), keep(bias.reshape(1, channels)),
    )

    gf, gwt, gb, out = pl.pallas_call(
        final_kernel,
        out_shape=(
            shape(block, BF16),
            shape((channels, inputs), F32),
            shape((1, channels), F32),
            shape((channels, nodes), BF16),
        ),
        in_specs=[in_vmem] * 7,
        out_specs=(in_vmem,) * 3 + (in_hbm,),
        scratch_shapes=[dma(())],
        compiler_params=params(16),
        name="final",
    )(own, fl, fr, fy, gwt, gb, out)
    return out, gf, gwt.T, gb.reshape(channels)


def solution(mesh):
    return jax.shard_map(
        local,
        mesh=mesh,
        in_specs=(
            P("feat", "node"),
            P(None, "feat"),
            P("feat"),
            P("node", None, None, None, None),
            P("node", None, None),
            P("node", None, None),
            P("node", None),
            P("feat", "node"),
        ),
        out_specs=(P("feat", "node"), P("feat", "node"), P(None, "feat"), P("feat")),
        check_vma=False,
    )
```
